32 devices in a mesh: dp: 4 (over z), ctx: 4 (over y, core), tensor: 2 (over x).
Axes of the slice: x: 2, y: 2, z: 4, core: 2. Of those that a mesh axis runs over, the one named last changes fastest.
Arguments:
- block_input: bfloat16 [4, 1024, 2560], P('dp', ('ctx', 'tensor')), may hold values from -6 to 6
- segment_ids: int32 [4, 1024], P('dp', 'ctx'), may hold values from 0 to 2, as said below
- output_grad: bfloat16 [4, 1024, 2560], P('dp', ('ctx', 'tensor')), may hold values from -6 to 6
- attention_gain: bfloat16 [2560], P(('dp', 'ctx')), may hold values from 0.25 to 1.75
- query_weight: bfloat16 [2560, 2560], P(('dp', 'ctx'), 'tensor'), may hold values from -0.125 to 0.125
- keyvalue_weight: bfloat16 [2560, 512], P(('dp', 'ctx'), 'tensor'), may hold values from -0.125 to 0.125
- output_weight: bfloat16 [2560, 2560], P('tensor', ('dp', 'ctx')), may hold values from -1 to 1
- output_bias: bfloat16 [2560], P(('dp', 'ctx')), may hold values from -1.796875 to 1.796875
- channel_gain: bfloat16 [2560], P(('dp', 'ctx')), may hold values from 0.25 to 1.75
- gate_weight: bfloat16 [2560, 7680], P(('dp', 'ctx'), 'tensor'), may hold values from -0.125 to 0.125
- up_weight: bfloat16 [2560, 7680], P(('dp', 'ctx'), 'tensor'), may hold values from -0.125 to 0.125
- down_weight: bfloat16 [7680, 2560], P('tensor', ('dp', 'ctx')), may hold values from -0.0625 to 0.0625
- gate_bias: bfloat16 [7680], P('tensor'), may hold values from -1.796875 to 1.796875
- up_bias: bfloat16 [7680], P('tensor'), may hold values from -1.796875 to 1.796875
- down_bias: bfloat16 [2560], P(('dp', 'ctx')), may hold values from -1.796875 to 1.796875
Outputs:
- block_output: bfloat16 [4, 1024, 2560], P('dp', ('ctx', 'tensor'))
- input_grad: float32 [4, 1024, 2560], P('dp', ('ctx', 'tensor'))
- attention_gain_grad: float32 [2560], P(('dp', 'ctx'))
- query_weight_grad: float32 [2560, 2560], P(('dp', 'ctx'), 'tensor')
- keyvalue_weight_grad: float32 [2560, 512], P(('dp', 'ctx'), 'tensor')
- output_weight_grad: float32 [2560, 2560], P('tensor', ('dp', 'ctx'))
- output_bias_grad: float32 [2560], P(('dp', 'ctx'))
- channel_gain_grad: float32 [2560], P(('dp', 'ctx'))
- gate_weight_grad: float32 [2560, 7680], P(('dp', 'ctx'), 'tensor')
- up_weight_grad: float32 [2560, 7680], P(('dp', 'ctx'), 'tensor')
- down_weight_grad: float32 [7680, 2560], P('tensor', ('dp', 'ctx'))
- gate_bias_grad: float32 [7680], P('tensor')
- up_bias_grad: float32 [7680], P('tensor')
- down_bias_grad: float32 [2560], P(('dp', 'ctx'))
The draws below stay inside these ranges and needn't reach their ends.
Inputs may be any that keep to these rules, and one draw needn't show every extreme that they name: `segment_ids`: within each sequence the numbers start at 0 and rise by 0 or 1 from one token to the next; every sequence holds exactly three documents. The first and the last have 256 // 4 to 255 tokens each (at least one), so that the middle one begins among the first 256 tokens and ends among the last 256 tokens.
All inputs are finite; a program needn't handle non-finite values.
Results may differ from the reference program's by a relative error of at most 0.014.
Values may be sent and summed in bfloat16 or wider, within the bound.
No kernel may reach another device: no remote copies, remote signals or barrier semaphores. Data moves between devices by JAX's collectives and lax.ppermute only.
A program may use at most 256 MiB of HBM per device.

```python
import math
import jax
import jax.numpy as jnp
from jax import lax

D = 2560
H = 10
HD = 256
FF = 7680
WINDOW = 2048
GROUP = 256
L = 1024
SEQS = 4


def draw_segment_ids(key, part):
    key = jax.random.fold_in(key, 7)
    first_key, last_key = jax.random.split(key, 2)
    shortest = max(1, GROUP // 4)
    token_index = jnp.arange(L, dtype=jnp.int32)[None, :]
    long_start = jax.random.randint(first_key, (SEQS, 1), shortest, GROUP)
    long_end = L - jax.random.randint(last_key, (SEQS, 1), shortest, GROUP)
    starts = (token_index == 0) | (token_index == long_start) | (token_index == long_end)
    return (jnp.cumsum(starts.astype(jnp.int32), axis=1) - 1).astype(jnp.int32)


def block_levels(rng, shape, shards, least, largest):
    def one(dim, blocks):
        steps = jax.random.uniform(jax.random.fold_in(jax.random.fold_in(rng, 6), dim), (blocks,), jnp.float32, least / len(shards), largest / len(shards))
        return jnp.repeat(jnp.exp(steps), shape[dim] // blocks).reshape((-1,) + (1,) * (len(shape) - dim - 1))

    factor_of = one(*shards[0])
    for cut in shards[1:]:
        factor_of = factor_of * one(*cut)
    return factor_of


def normal_values(key, extent, width, bound, cuts=(), kind=jnp.bfloat16):
    entries = jax.random.normal(key, extent, jnp.float32) * width
    if len(cuts) > 0:
        entries = block_levels(key, extent, cuts, -0.22, 0.18) * entries
    return jnp.clip(entries, min=-bound, max=bound).astype(kind)


def setup_inputs(seed: int = 0) -> dict:
    splits = jax.random.split(jax.random.key(seed), 16)
    block_input = normal_values(splits[0], (SEQS, L, D), 1.0, 6.0, ((0, 4), (1, 8)))
    segment_ids = draw_segment_ids(jax.random.fold_in(splits[15], 71), 0)
    output_grad = normal_values(splits[2], (SEQS, L, D), 1.0, 6.0, ((0, 4), (1, 8)))
    attention_gain = jnp.clip(1.0 + 0.15 * jax.random.normal(splits[3], (D,), jnp.float32), 0.25, 1.75).astype(jnp.bfloat16)
    query_weight = normal_values(splits[4], (D, H * HD), D ** -0.5, 0.125, ((0, 16), (1, 2)))
    keyvalue_weight = normal_values(splits[5], (D, 2 * HD), D ** -0.5, 0.125, ((0, 16), (1, 2)))
    output_weight = normal_values(splits[6], (H * HD, D), (H * HD // 64) ** -0.5, 1.0, ((0, 2), (1, 16)))
    output_bias = normal_values(splits[7], (D,), 0.3, 1.796875, ((0, 16),))
    channel_gain = jnp.clip(1.0 + 0.15 * jax.random.normal(splits[8], (D,), jnp.float32), 0.25, 1.75).astype(jnp.bfloat16)
    gate_weight = normal_values(splits[9], (D, FF), D ** -0.5, 0.125, ((0, 16), (1, 2)))
    up_weight = normal_values(splits[10], (D, FF), D ** -0.5, 0.125, ((0, 16), (1, 2)))
    down_weight = normal_values(splits[11], (FF, D), FF ** -0.5, 0.0625, ((0, 2), (1, 16)))
    gate_bias = normal_values(splits[12], (FF,), 0.3, 1.796875, ((0, 2),))
    up_bias = normal_values(splits[13], (FF,), 0.3, 1.796875, ((0, 2),))
    down_bias = normal_values(splits[14], (D,), 0.3, 1.796875, ((0, 16),))
    return dict(block_input=block_input, segment_ids=segment_ids, output_grad=output_grad, attention_gain=attention_gain, query_weight=query_weight, keyvalue_weight=keyvalue_weight, output_weight=output_weight, output_bias=output_bias, channel_gain=channel_gain, gate_weight=gate_weight, up_weight=up_weight, down_weight=down_weight, gate_bias=gate_bias, up_bias=up_bias, down_bias=down_bias)


@jax.custom_vjp
def low(v):
    return lax.optimization_barrier(v.astype(jnp.bfloat16)).astype(jnp.float32)

@jax.custom_vjp
def low_back(v):
    return v

def low_keep(v):
    return (low(v), None)

def low_pass(kept, grad):
    return (grad,)

def back_keep(v):
    return (v, None)

def back_low(kept, grad):
    return (low(grad),)
low.defvjp(low_keep, low_pass)
low_back.defvjp(back_keep, back_low)

def dot_high(left, right):
    return jnp.dot(left, right, precision=lax.Precision.HIGHEST)

def norm_scale(vectors, scale_gain):
    return vectors * lax.rsqrt(lax.optimization_barrier(jnp.mean(vectors * vectors, axis=-1, keepdims=True)) + 1e-06) * scale_gain

def rotary_tables(positions, head_size):
    quarter = head_size // 4
    frequency = jnp.exp(jnp.arange(quarter, dtype=jnp.float32) * (-math.log(10000.0) / quarter))
    angles = positions.astype(jnp.float32)[:, None] * frequency[None, :]
    return (jnp.cos(angles), jnp.sin(angles))

def rotate(vectors, cosine_table, sine_table, direction):
    quarter = cosine_table.shape[-1]
    lead_part = vectors[..., :quarter]
    trail_part = vectors[..., quarter:2 * quarter]
    cosine_wide = cosine_table[:, None, :]
    sine_wide = direction * sine_table[:, None, :]
    return jnp.concatenate([lead_part * cosine_wide - trail_part * sine_wide, trail_part * cosine_wide + lead_part * sine_wide, vectors[..., 2 * quarter:]], axis=-1)

def doc_positions(seq_segments):
    token_index = jnp.arange(seq_segments.shape[0], dtype=jnp.int32)
    is_first = jnp.concatenate([jnp.ones((1,), dtype=bool), seq_segments[1:] != seq_segments[:-1]])
    first_index = lax.cummax(jnp.where(is_first, token_index, jnp.zeros_like(token_index)))
    return token_index - first_index

def one_sequence(weights, pair):
    attention_gain, query_weight, keyvalue_weight, output_weight, output_bias, channel_gain, gate_weight, up_weight, down_weight, gate_bias, up_bias, down_bias = weights
    seq_input, seq_segments = pair
    length = seq_input.shape[0]
    head_count = query_weight.shape[1] // HD
    positions = doc_positions(seq_segments)
    cosine_table, sine_table = rotary_tables(positions, HD)
    normed = low(norm_scale(seq_input, attention_gain))
    query_proj = low_back(dot_high(normed, query_weight))
    queries = low(rotate(query_proj.reshape(length, head_count, HD), cosine_table, sine_table, 1.0) * HD ** (-0.5))
    keyvalue_proj = low_back(dot_high(normed, keyvalue_weight))
    all_keys = low(rotate(keyvalue_proj[:, None, :HD], cosine_table, sine_table, 1.0)[:, 0])
    all_values = low(keyvalue_proj[:, HD:])
    token_index = jnp.arange(length, dtype=jnp.int32)
    allowed = (seq_segments[:, None] == seq_segments[None, :]) & (token_index[None, :] <= token_index[:, None]) & (token_index[:, None] - token_index[None, :] < WINDOW)
    scores = low_back(jnp.einsum('qhd,kd->hqk', queries, all_keys, precision=lax.Precision.HIGHEST))
    scores = jnp.where(allowed[None], scores, -1e+30)
    score_peak = lax.optimization_barrier(jnp.max(scores, axis=-1, keepdims=True))
    exp_scores = jnp.exp(scores - score_peak)
    attn_probs = exp_scores / lax.optimization_barrier(jnp.sum(exp_scores, axis=-1, keepdims=True))
    context = low(low_back(jnp.einsum('hqk,kd->qhd', low(attn_probs), all_values, precision=lax.Precision.HIGHEST)))
    attended = low_back(dot_high(context.reshape(length, head_count * HD), output_weight))
    mixed = seq_input + attended + output_bias
    normed_two = low(norm_scale(mixed, channel_gain))
    gate_pre = low_back(dot_high(normed_two, gate_weight)) + gate_bias
    up_pre = low_back(dot_high(normed_two, up_weight)) + up_bias
    hidden = low(jax.nn.gelu(gate_pre, approximate=True) * up_pre)
    return mixed + low_back(dot_high(hidden, down_weight)) + down_bias

def reference(block_input, segment_ids, output_grad, attention_gain, query_weight, keyvalue_weight, output_weight, output_bias, channel_gain, gate_weight, up_weight, down_weight, gate_bias, up_bias, down_bias):
    weights = tuple((item.astype(jnp.float32) for item in (attention_gain, query_weight, keyvalue_weight, output_weight, output_bias, channel_gain, gate_weight, up_weight, down_weight, gate_bias, up_bias, down_bias)))
    inputs = block_input.astype(jnp.float32)

    def forward(seq_inputs, params):

        def seq_step(pair):
            return one_sequence(params, pair)
        return lax.map(jax.checkpoint(seq_step), (seq_inputs, segment_ids))
    outputs, pullback = jax.vjp(forward, inputs, weights)
    input_grad, grads = pullback(output_grad.astype(jnp.float32))
    gain_one_grad, query_grad, keyvalue_grad, proj_grad, obias_grad, gain_two_grad, gate_wgrad, up_wgrad, down_wgrad, gbias_grad, ubias_grad, dbias_grad = grads
    return (outputs.astype(jnp.bfloat16), input_grad, gain_one_grad, query_grad, keyvalue_grad, proj_grad, obias_grad, gain_two_grad, gate_wgrad, up_wgrad, down_wgrad, gbias_grad, ubias_grad, dbias_grad)
```

```python
from functools import partial
import math

import jax
import jax.numpy as jnp
from jax import lax
from jax.sharding import PartitionSpec as P

HD = 256
WINDOW = 2048
LANES = 128
f32 = jnp.float32
bf16 = jnp.bfloat16


def norm_scale(vectors, scale_gain):
    return (
        vectors
        * lax.rsqrt(jnp.mean(vectors * vectors, axis=-1, keepdims=True) + 1e-06)
        * scale_gain
    )


def rotary_tables(positions, head_size):
    quarter = head_size // 4
    frequency = jnp.exp(jnp.arange(quarter, dtype=jnp.float32) * (-math.log(10000.0) / quarter))
    angles = positions.astype(jnp.float32)[:, None] * frequency[None, :]
    return (jnp.cos(angles), jnp.sin(angles))


def rotate(vectors, cosine_table, sine_table, direction):
    quarter = cosine_table.shape[-1]
    lead_part = vectors[..., :quarter]
    trail_part = vectors[..., quarter : 2 * quarter]
    cosine_wide = cosine_table[:, None, :]
    sine_wide = direction * sine_table[:, None, :]
    return jnp.concatenate(
        [
            lead_part * cosine_wide - trail_part * sine_wide,
            trail_part * cosine_wide + lead_part * sine_wide,
            vectors[..., 2 * quarter :],
        ],
        axis=-1,
    )


def bits_of(axis, size):
    masks = []
    while size > 1:
        size //= 2
        masks.append((axis, size))
    return masks


def swap(values, bit):
    axis, mask = bit
    return lax.ppermute(values, axis, [(i, i ^ mask) for i in range(lax.axis_size(axis))])


def digit(bit):
    axis, mask = bit
    return (lax.axis_index(axis) // mask) % 2


def in_order(bit, mine, other):
    one = digit(bit) == 1
    return jnp.where(one, other, mine), jnp.where(one, mine, other)


def halves(values, bit, axis):
    size = values.shape[axis] // 2
    own = digit(bit)
    return (
        lax.dynamic_slice_in_dim(values, own * size, size, axis),
        lax.dynamic_slice_in_dim(values, (1 - own) * size, size, axis),
    )


class Plan:
    def __init__(self, sizes, shared):
        dp = bits_of("dp", sizes["dp"])
        ctx = bits_of("ctx", sizes["ctx"])
        self.sizes = sizes
        self.rows = dp + ctx
        self.ctx = ctx
        self.dp = dp
        self.tensor = bits_of("tensor", sizes["tensor"])[0]
        cut = len(dp) - shared
        self.repeat = dp[:cut]
        self.split = ctx + dp[cut:]
        self.core = ctx[-1]
        self.links = [self.tensor] + ctx[:-1] + dp[cut:]

    def where(self, bit, present):
        return sum(1 for other in self.rows[: self.rows.index(bit)] if other in present)


def spread_in(shard, plan):
    present = []
    for bit in plan.split:
        mine, theirs = halves(shard, bit, shard.ndim - 1)
        place = plan.where(bit, present)
        shard = jnp.stack(in_order(bit, mine, swap(theirs, bit)), axis=place)
        present.append(bit)
    for bit in plan.repeat:
        place = plan.where(bit, present)
        shard = jnp.stack(in_order(bit, shard, swap(shard, bit)), axis=place)
        present.append(bit)
    return shard.reshape(-1, shard.shape[-1])


def spread_out(grad, plan):
    columns = grad.shape[-1]
    grad = grad.reshape((2,) * len(plan.rows) + (-1, columns))
    present = list(plan.rows)
    for bit in plan.repeat:
        place = present.index(bit)
        present.remove(bit)
        mine, theirs = halves(grad, bit, place)
        grad = mine.astype(f32) + swap(theirs.astype(bf16), bit).astype(f32)
        grad = jnp.squeeze(grad, place).astype(bf16)
    for bit in reversed(plan.split):
        place = present.index(bit)
        present.remove(bit)
        mine, theirs = halves(grad, bit, place)
        grad = jnp.concatenate(in_order(bit, mine, swap(theirs, bit)), axis=-1)
        grad = jnp.squeeze(grad, place)
    return grad


def reduce_rows(grad, plan, order, kind=bf16):
    columns = grad.shape[-1]
    grad = grad.reshape((2,) * len(plan.rows) + (-1, columns))
    present = list(plan.rows)
    for bit in order:
        place = present.index(bit)
        present.remove(bit)
        mine, theirs = halves(grad, bit, place)
        grad = mine.astype(f32) + swap(theirs.astype(kind), bit).astype(f32)
        grad = jnp.squeeze(grad, place)
        if present:
            grad = grad.astype(kind)
    return grad


def token_parts(count, plan):
    links = len(plan.links)
    step = 16
    units = count // step
    sizes = [(units // links + (1 if i < units % links else 0)) * step for i in range(links)]
    parts = []
    start = 0
    for i, size in enumerate(sizes):
        if size:
            parts.append((start, size, plan.links[i:] + plan.links[:i]))
            start += size
    return parts


def gather_tokens(local_rows, plan):
    pieces = []
    for start, size, order in token_parts(local_rows.shape[0], plan):
        piece = local_rows[start : start + size]
        for bit in order:
            piece = jnp.concatenate([piece, swap(piece, bit)], axis=0)
        pieces.append(piece)
    chip = jnp.concatenate(pieces, axis=0)
    return jnp.concatenate([chip, swap(chip, plan.core)], axis=0)


def reduce_tokens(partial_rows, plan, count):
    size = partial_rows.shape[0] // 2
    chip = partial_rows[:size].astype(f32) + swap(
        partial_rows[size:].astype(bf16), plan.core
    ).astype(f32)
    chip = chip.astype(bf16)
    pieces = []
    copies = size // count
    for start, size, order in token_parts(count, plan):
        piece = chip[start * copies : (start + size) * copies]
        for bit in reversed(order):
            half = piece.shape[0] // 2
            piece = piece[:half].astype(f32) + swap(piece[half:].astype(bf16), bit).astype(f32)
            if half > size:
                piece = piece.astype(bf16)
        pieces.append(piece)
    return jnp.concatenate(pieces, axis=0)


def gather_rows(values_low, plan):
    return jnp.concatenate(in_order(plan.tensor, values_low, swap(values_low, plan.tensor)), axis=0)


def sum_rows(partial_rows, plan):
    mine, theirs = halves(partial_rows, plan.tensor, 0)
    return mine.astype(f32) + swap(theirs.astype(bf16), plan.tensor).astype(f32)


def local(
    plan,
    block_input,
    segment_ids,
    output_grad,
    attention_gain,
    query_weight,
    keyvalue_weight,
    output_weight,
    output_bias,
    channel_gain,
    gate_weight,
    up_weight,
    down_weight,
    gate_bias,
    up_bias,
    down_bias,
):
    local_in = block_input[0].astype(f32)
    grad_local = output_grad[0]
    tensor_index = lax.axis_index("tensor")
    ctx_index = lax.axis_index("ctx")
    is_key = tensor_index == 0
    shard_rows = attention_gain.shape[0]
    token_count, width = local_in.shape
    ff_half = gate_bias.shape[0]
    blocks = 2 ** len(plan.split)
    block = -(-ff_half // (blocks * LANES)) * LANES
    ff_pad = blocks * block - ff_half

    vectors = jnp.stack([attention_gain, output_bias, channel_gain, down_bias], axis=1)
    vectors = jnp.pad(vectors, ((0, 0), (0, LANES - 4)))
    first = lax.all_gather(
        jnp.concatenate([keyvalue_weight, vectors], axis=1), ("dp", "ctx"), axis=0, tiled=True
    )
    full_keyvalue = first[:, : keyvalue_weight.shape[1]]
    vectors = first[:, keyvalue_weight.shape[1] :].astype(f32)
    gain_one, full_obias, gain_two, full_dbias = (vectors[:, i] for i in range(4))
    full_query = lax.all_gather(query_weight, ("dp", "ctx"), axis=0, tiled=True)
    full_output = lax.all_gather(output_weight.T, ("dp", "ctx"), axis=0, tiled=True)

    pad = ((0, 0), (0, ff_pad))
    full_gate = spread_in(jnp.pad(gate_weight, pad), plan)
    full_up = spread_in(jnp.pad(up_weight, pad), plan)
    full_down = spread_in(jnp.pad(down_weight.T, pad), plan)
    block_index = 0
    for bit in plan.split:
        block_index = block_index * 2 + digit(bit)
    gate_bias_block, up_bias_block = (
        lax.dynamic_slice_in_dim(jnp.pad(item, (0, ff_pad)), block_index * block, block).astype(f32)
        for item in (gate_bias, up_bias)
    )

    normed_local, norm_one_pull = jax.vjp(norm_scale, local_in, gain_one)
    normed = gather_rows(normed_local.astype(bf16), plan)
    row_count = normed.shape[0]
    all_segments = lax.all_gather(segment_ids, "ctx", axis=1, tiled=True)[0]
    length = all_segments.shape[0]
    own_segments = lax.dynamic_slice_in_dim(all_segments, ctx_index * row_count, row_count)
    query_index = ctx_index * row_count + jnp.arange(row_count, dtype=jnp.int32)
    earlier = jnp.sum((all_segments[None, :] < own_segments[:, None]).astype(jnp.int32), axis=1)
    cosine_table, sine_table = rotary_tables(query_index - earlier, HD)
    head_count = full_query.shape[1] // HD
    half_proj = jnp.dot(normed, full_keyvalue, preferred_element_type=f32)
    half_low = jnp.where(
        is_key, rotate(half_proj[:, None, :], cosine_table, sine_table, 1.0)[:, 0], half_proj
    ).astype(bf16)
    keyvalue = jnp.concatenate(in_order(plan.tensor, half_low, swap(half_low, plan.tensor)), axis=1)
    masks = [0]
    for bit in plan.ctx:
        keyvalue = jnp.concatenate([keyvalue, swap(keyvalue, bit)], axis=0)
        masks = masks + [mask ^ bit[1] for mask in masks]
    all_keys = keyvalue[:, :HD]
    all_values = keyvalue[:, HD:]
    key_index = jnp.concatenate(
        [(ctx_index ^ mask) * row_count + jnp.arange(row_count, dtype=jnp.int32) for mask in masks]
    )
    key_segments = jnp.concatenate(
        [
            lax.dynamic_slice_in_dim(all_segments, (ctx_index ^ mask) * row_count, row_count)
            for mask in masks
        ]
    )
    query_proj = jnp.dot(normed, full_query, preferred_element_type=f32)
    queries = (
        rotate(query_proj.reshape(row_count, head_count, HD), cosine_table, sine_table, 1.0)
        * HD ** (-0.5)
    ).astype(bf16)
    allowed = (
        (own_segments[:, None] == key_segments[None, :])
        & (key_index[None, :] <= query_index[:, None])
        & (query_index[:, None] - key_index[None, :] < WINDOW)
    )
    scores = jnp.einsum("qhd,kd->hqk", queries, all_keys, preferred_element_type=f32)
    scores = jnp.where(allowed[None], scores, -1e30)
    score_peak = jnp.max(scores, axis=-1, keepdims=True)
    exp_scores = jnp.exp(scores - score_peak)
    exp_total = jnp.sum(exp_scores, axis=-1, keepdims=True)
    probs = exp_scores / exp_total
    probs_low = probs.astype(bf16)
    context = jnp.einsum("hqk,kd->qhd", probs_low, all_values, preferred_element_type=f32)
    context = context.astype(bf16).reshape(row_count, head_count * HD)
    attended = jnp.einsum("rc,dc->rd", context, full_output, preferred_element_type=f32)
    mixed = local_in + sum_rows(attended, plan) + full_obias

    grad_full = grad_local.astype(f32)
    dbias_part = jnp.sum(grad_full, axis=0)
    grad_rows = gather_tokens(grad_local, plan)
    hidden_grad = jnp.dot(grad_rows, full_down, preferred_element_type=f32)
    normed_two_local, norm_two_pull = jax.vjp(norm_scale, mixed, gain_two)
    normed_two = gather_tokens(normed_two_local.astype(bf16), plan)
    gate_pre = jnp.dot(normed_two, full_gate, preferred_element_type=f32) + gate_bias_block
    up_pre = jnp.dot(normed_two, full_up, preferred_element_type=f32) + up_bias_block
    activated, gelu_pull = jax.vjp(partial(jax.nn.gelu, approximate=True), gate_pre)
    hidden = (activated * up_pre).astype(bf16)
    gate_grad_full = gelu_pull(hidden_grad * up_pre)[0]
    up_grad_full = hidden_grad * activated
    gbias_part = jnp.sum(gate_grad_full, axis=0)
    ubias_part = jnp.sum(up_grad_full, axis=0)
    gate_grad = gate_grad_full.astype(bf16)
    up_grad = up_grad_full.astype(bf16)
    two_part = jnp.einsum(
        "rf,df->rd", gate_grad, full_gate, preferred_element_type=f32
    ) + jnp.einsum("rf,df->rd", up_grad, full_up, preferred_element_type=f32)
    two_grad = reduce_tokens(two_part.astype(bf16), plan, token_count)
    out_part = jnp.einsum("rf,df->rd", hidden, full_down, preferred_element_type=f32)
    block_output = (
        mixed + reduce_tokens(out_part.astype(bf16), plan, token_count) + full_dbias
    ).astype(bf16)
    ff_grads = []
    for rows, branch in ((grad_rows, hidden), (normed_two, gate_grad), (normed_two, up_grad)):
        weight_grad = jnp.einsum("rd,rf->df", rows, branch, preferred_element_type=f32)
        ff_grads.append(spread_out(weight_grad.astype(bf16), plan)[:, :ff_half].astype(f32))
    down_out, gate_out, up_out = ff_grads

    mixed_part, gain_two_part = norm_two_pull(two_grad)
    mixed_grad = grad_full + mixed_part
    obias_part = jnp.sum(mixed_grad, axis=0)
    attn_rows = gather_rows(mixed_grad.astype(bf16), plan)
    order = plan.ctx[::-1] + plan.dp[::-1]
    output_wgrad = jnp.einsum("rd,rc->dc", attn_rows, context, preferred_element_type=f32)
    proj_out = reduce_rows(output_wgrad.astype(bf16), plan, order)
    context_grad = jnp.dot(attn_rows, full_output, preferred_element_type=f32).astype(bf16)
    context_grad = context_grad.reshape(row_count, head_count, HD)
    probs_grad = jnp.einsum("qhd,kd->hqk", context_grad, all_values, preferred_element_type=f32)
    values_grad = jnp.einsum("hqk,qhd->kd", probs_low, context_grad, preferred_element_type=f32)
    prob_dot = jnp.sum(probs * probs_grad, axis=-1, keepdims=True)
    score_grad = (probs * (probs_grad - prob_dot)).astype(bf16)
    query_grad = jnp.einsum("hqk,kd->qhd", score_grad, all_keys, preferred_element_type=f32)
    keys_grad = jnp.einsum("hqk,qhd->kd", score_grad, queries, preferred_element_type=f32)
    stacked = jnp.concatenate([keys_grad, values_grad], axis=1)
    for bit in reversed(plan.ctx):
        half = stacked.shape[0] // 2
        stacked = stacked[:half] + swap(stacked[half:].astype(bf16), bit).astype(f32)
    mine, theirs = halves(stacked, plan.tensor, 1)
    half_grad = mine + swap(theirs.astype(bf16), plan.tensor).astype(f32)
    half_grad = jnp.where(
        is_key, rotate(half_grad[:, None, :], cosine_table, sine_table, -1.0)[:, 0], half_grad
    ).astype(bf16)
    query_proj_grad = rotate(query_grad * HD ** (-0.5), cosine_table, sine_table, -1.0)
    query_proj_grad = query_proj_grad.reshape(row_count, head_count * HD).astype(bf16)
    query_wgrad = jnp.einsum("rd,rc->dc", normed, query_proj_grad, preferred_element_type=f32)
    query_out = reduce_rows(query_wgrad.astype(bf16), plan, order)
    keyvalue_wgrad = jnp.einsum("rd,rc->dc", normed, half_grad, preferred_element_type=f32)
    keyvalue_out = reduce_rows(keyvalue_wgrad.astype(bf16), plan, order)
    one_part = jnp.einsum(
        "rc,dc->rd", query_proj_grad, full_query, preferred_element_type=f32
    ) + jnp.einsum("rc,dc->rd", half_grad, full_keyvalue, preferred_element_type=f32)
    input_part, gain_one_part = norm_one_pull(sum_rows(one_part, plan))
    input_grad = mixed_grad + input_part

    small = jnp.stack([gain_one_part, gain_two_part, obias_part, dbias_part], axis=0)
    small = small.reshape(4, -1, shard_rows).transpose(1, 0, 2)
    small = small + swap(small, plan.tensor)
    small = reduce_rows(small.reshape(-1, shard_rows), plan, order, f32)
    ff_small = jnp.stack([gbias_part, ubias_part], axis=0)
    for bit in plan.repeat:
        ff_small = ff_small + swap(ff_small, bit)
    for bit in reversed(plan.split):
        ff_small = jnp.concatenate(in_order(bit, ff_small, swap(ff_small, bit)), axis=1)
    return (
        block_output[None],
        input_grad[None],
        small[0],
        query_out,
        keyvalue_out,
        proj_out.T,
        small[2],
        small[1],
        gate_out,
        up_out,
        down_out.T,
        ff_small[0, :ff_half],
        ff_small[1, :ff_half],
        small[3],
    )


SHARED = 1


def solution(mesh):
    plan = Plan(dict(mesh.shape), SHARED)
    rows = P("dp", ("ctx", "tensor"), None)
    vector = P(("dp", "ctx"))
    wide = P(("dp", "ctx"), "tensor")
    tall = P("tensor", ("dp", "ctx"))
    units = P("tensor")
    return jax.shard_map(
        partial(local, plan),
        mesh=mesh,
        in_specs=(
            rows,
            P("dp", "ctx"),
            rows,
            vector,
            wide,
            wide,
            tall,
            vector,
            vector,
            wide,
            wide,
            tall,
            units,
            units,
            vector,
        ),
        out_specs=(
            rows,
            rows,
            vector,
            wide,
            wide,
            tall,
            vector,
            vector,
            wide,
            wide,
            tall,
            units,
            units,
            vector,
        ),
        check_vma=False,
    )
```

```python
from functools import partial
import math

import jax
import jax.numpy as jnp
from jax import lax
from jax.sharding import Mesh
from jax.sharding import PartitionSpec as P

HD = 256
WINDOW = 2048
LANES = 128
DP = ("far", "near")
CTX = ("y", "core")
DP_CTX = DP + CTX
f32 = jnp.float32
bf16 = jnp.bfloat16


def norm_scale(vectors, scale_gain):
    return (
        vectors
        * lax.rsqrt(jnp.mean(vectors * vectors, axis=-1, keepdims=True) + 1e-06)
        * scale_gain
    )


def rotary_tables(positions, head_size):
    quarter = head_size // 4
    frequency = jnp.exp(jnp.arange(quarter, dtype=jnp.float32) * (-math.log(10000.0) / quarter))
    angles = positions.astype(jnp.float32)[:, None] * frequency[None, :]
    return (jnp.cos(angles), jnp.sin(angles))


def rotate(vectors, cosine_table, sine_table, direction):
    quarter = cosine_table.shape[-1]
    lead_part = vectors[..., :quarter]
    trail_part = vectors[..., quarter : 2 * quarter]
    cosine_wide = cosine_table[:, None, :]
    sine_wide = direction * sine_table[:, None, :]
    return jnp.concatenate(
        [
            lead_part * cosine_wide - trail_part * sine_wide,
            trail_part * cosine_wide + lead_part * sine_wide,
            vectors[..., 2 * quarter :],
        ],
        axis=-1,
    )


def bits_of(axis, size):
    masks = []
    while size > 1:
        size //= 2
        masks.append((axis, size))
    return masks


def swap(values, bit):
    axis, mask = bit
    return lax.ppermute(values, axis, [(i, i ^ mask) for i in range(lax.axis_size(axis))])


def digit(bit):
    axis, mask = bit
    return (lax.axis_index(axis) // mask) % 2


def in_order(bit, mine, other):
    one = digit(bit) == 1
    return jnp.where(one, other, mine), jnp.where(one, mine, other)


def halves(values, bit, axis):
    size = values.shape[axis] // 2
    own = digit(bit)
    return (
        lax.dynamic_slice_in_dim(values, own * size, size, axis),
        lax.dynamic_slice_in_dim(values, (1 - own) * size, size, axis),
    )


def tie(*groups):
    return lax.optimization_barrier(groups)


def tie_to(values, hold):
    return (values, None) if hold is None else tie(values, hold)


class Plan:
    def __init__(self, sizes):
        self.far = bits_of("far", sizes["far"])
        self.near = bits_of("near", sizes["near"])
        self.y = bits_of("y", sizes["y"])
        self.core = ("core", 1)
        self.tensor = ("tensor", 1)
        self.ctx = self.y + [self.core]
        self.rows = self.far + self.near + self.ctx
        self.links = [self.tensor] + self.y + self.near
        self.chip = self.near + self.y + [self.tensor]
        self.blocks = sizes["near"] * sizes["y"] * 2


class Journey:
    def __init__(self, steps):
        self.steps = steps
        self.result = None
        next(steps)

    def step(self, hold):
        try:
            return self.steps.send(hold)
        except StopIteration as end:
            self.result, hold = end.value
            return hold

    def finish(self, hold):
        while self.result is None:
            hold = self.step(hold)
        return hold


def repeat_in(arrays, plan, cuts):
    hold, whole = None, []
    for rows in arrays:
        size = rows.shape[0] // cuts
        pieces = []
        for start in range(0, rows.shape[0], size):
            piece = rows[start : start + size]
            if hold is not None:
                piece, hold = tie(piece, hold)
            for bit in reversed(plan.far):
                other = swap(piece, bit)
                hold = yield hold
                other, hold = tie_to(other, hold)
                piece = jnp.concatenate(in_order(bit, piece, other), axis=0)
            pieces.append(piece.reshape(-1, size, rows.shape[1]))
        whole.append(jnp.concatenate(pieces, axis=1).reshape(-1, rows.shape[1]))
    return whole, hold


def spread_out(grad, plan):
    grad = lax.psum_scatter(grad, "far", scatter_dimension=0, tiled=True)
    hold = yield None
    grad, hold = tie_to(grad, hold)
    bits = plan.near + plan.ctx
    grad = grad.reshape((2,) * len(bits) + (-1, grad.shape[-1]))
    for bit in reversed(bits):
        place = grad.ndim - 3
        mine, theirs = halves(grad, bit, place)
        other = swap(theirs, bit)
        hold = yield hold
        other, hold = tie_to(other, hold)
        grad = jnp.squeeze(jnp.concatenate(in_order(bit, mine, other), axis=-1), place)
    return grad, hold


def reduce_rows(grads, plan, orders, kind=bf16):
    hold = None
    states = [
        (grad.reshape((2,) * len(plan.rows) + (-1, grad.shape[-1])), list(plan.rows))
        for grad in grads
    ]
    for step in range(len(plan.rows)):
        kept, others = [], []
        for (grad, present), order in zip(states, orders, strict=True):
            place = present.index(order[step])
            mine, theirs = halves(grad, order[step], place)
            kept.append((jnp.squeeze(mine, place), present[:place] + present[place + 1 :]))
            others.append(jnp.squeeze(swap(theirs.astype(kind), order[step]), place))
        hold = yield hold
        others, hold = tie_to(others, hold)
        states = []
        for (mine, present), other in zip(kept, others, strict=True):
            grad = mine.astype(f32) + other.astype(f32)
            states.append((grad.astype(kind) if present else grad, present))
    return [grad for grad, _ in states], hold


def spread_small(part, plan):
    hold = None
    for bit in plan.far:
        other = swap(part, bit)
        hold = yield hold
        other, hold = tie_to(other, hold)
        part = part + other
    for bit in reversed(plan.near + plan.ctx):
        other = swap(part, bit)
        hold = yield hold
        other, hold = tie_to(other, hold)
        part = jnp.concatenate(in_order(bit, part, other), axis=1)
    return part, hold


def token_parts(count, plan):
    links = len(plan.links)
    step = 16
    units = count // step
    sizes = [(units // links + (1 if i < units % links else 0)) * step for i in range(links)]
    parts = []
    start = 0
    for i, size in enumerate(sizes):
        if size:
            parts.append((start, size, plan.links[i:] + plan.links[:i]))
            start += size
    return parts


def gather_tokens(local_rows, plan):
    hold = None
    parts = token_parts(local_rows.shape[0], plan)
    pieces = [(local_rows[start : start + size], []) for start, size, _ in parts]
    for step in range(len(plan.links)):
        bits = [order[step] for _, _, order in parts]
        others = [swap(piece, bit) for (piece, _), bit in zip(pieces, bits, strict=True)]
        hold = yield hold
        others, hold = tie_to(others, hold)
        grown = []
        for (piece, present), bit, other in zip(pieces, bits, others, strict=True):
            place = sum(1 for done in present if plan.chip.index(done) < plan.chip.index(bit))
            grown.append((jnp.stack(in_order(bit, piece, other), axis=place), present + [bit]))
        pieces = grown
    chip = jnp.concatenate([piece for piece, _ in pieces], axis=-2).reshape(
        -1, local_rows.shape[1]
    )
    return [chip, swap(chip, plan.core)], hold


def reduce_tokens(own, other, plan, count):
    got = swap(other, plan.core)
    hold = yield None
    got, hold = tie_to(got, hold)
    chip = (own.astype(f32) + got.astype(f32)).astype(bf16)
    chip = chip.reshape((2,) * len(plan.chip) + (count, -1))
    parts = token_parts(count, plan)
    pieces = [
        (lax.slice_in_dim(chip, start, start + size, axis=chip.ndim - 2), list(plan.chip))
        for start, size, _ in parts
    ]
    for step in reversed(range(len(plan.links))):
        kept, others = [], []
        for (piece, present), (_, _, order) in zip(pieces, parts, strict=True):
            place = present.index(order[step])
            mine, theirs = halves(piece, order[step], place)
            kept.append((jnp.squeeze(mine, place), present[:place] + present[place + 1 :]))
            others.append(swap(jnp.squeeze(theirs, place), order[step]))
        hold = yield hold
        others, hold = tie_to(others, hold)
        pieces = []
        for (mine, present), got in zip(kept, others, strict=True):
            piece = mine.astype(f32) + got.astype(f32)
            pieces.append((piece.astype(bf16) if present else piece, present))
    return jnp.concatenate([piece for piece, _ in pieces], axis=0), hold


def gather_rows(values_low, plan):
    return jnp.concatenate(in_order(plan.tensor, values_low, swap(values_low, plan.tensor)), axis=0)


def sum_rows(partial_rows, plan):
    mine, theirs = halves(partial_rows, plan.tensor, 0)
    return mine.astype(f32) + swap(theirs.astype(bf16), plan.tensor).astype(f32)


def local(
    plan,
    block_input,
    segment_ids,
    output_grad,
    attention_gain,
    query_weight,
    keyvalue_weight,
    output_weight,
    output_bias,
    channel_gain,
    gate_weight,
    up_weight,
    down_weight,
    gate_bias,
    up_bias,
    down_bias,
):
    local_in = block_input[0].astype(f32)
    grad_local = output_grad[0]
    is_key = lax.axis_index("tensor") == 0
    ctx_index = lax.axis_index("y") * 2 + lax.axis_index("core")
    shard_rows = attention_gain.shape[0]
    token_count, width = local_in.shape
    ff_half = gate_bias.shape[0]
    blocks = plan.blocks
    block = -(-ff_half // (blocks * LANES)) * LANES
    ff_pad = blocks * block - ff_half

    segments = segment_ids[0]
    row_count = segments.shape[0]
    offsets = [0]
    for axis, mask in plan.ctx:
        segments = jnp.concatenate([segments, swap(segments, (axis, mask))])
        offsets = offsets + [item ^ (mask * 2 if axis == "y" else mask) for item in offsets]
    piece_index = jnp.arange(row_count, dtype=jnp.int32)
    key_index = jnp.concatenate([(ctx_index ^ item) * row_count + piece_index for item in offsets])
    own_segments = segments[:row_count]
    query_index = key_index[:row_count]
    earlier = jnp.sum((segments[None, :] < own_segments[:, None]).astype(jnp.int32), axis=1)
    cosine_table, sine_table = rotary_tables(query_index - earlier, HD)
    allowed = (
        (own_segments[:, None] == segments[None, :])
        & (key_index[None, :] <= query_index[:, None])
        & (query_index[:, None] - key_index[None, :] < WINDOW)
    )

    def by_block(item):
        return lax.all_to_all(
            jnp.pad(item, ((0, 0), (0, ff_pad))),
            ("near",) + CTX,
            split_axis=1,
            concat_axis=0,
            tiled=True,
        )

    raw = block_input[0]
    raw_other = swap(raw, plan.tensor)
    down_rows, gate_rows, up_rows = (
        by_block(item) for item in (down_weight.T, gate_weight, up_weight)
    )

    vectors = jnp.stack([attention_gain, output_bias, channel_gain, down_bias], axis=1)
    vectors = jnp.pad(vectors, ((0, 0), (0, LANES - 4)))
    first = lax.all_gather(
        jnp.concatenate([query_weight, keyvalue_weight, vectors], axis=1),
        DP_CTX,
        axis=0,
        tiled=True,
    )
    full_output = lax.all_gather(output_weight.T, DP_CTX, axis=0, tiled=True)

    first, raw_other, *ff_rows = tie(first, raw_other, down_rows, gate_rows, up_rows)
    ff_in = Journey(repeat_in(ff_rows, plan, 2))
    block_start = (lax.axis_index("near") * (blocks // 2) + ctx_index) * block
    pair_bias = jnp.concatenate(
        [
            lax.dynamic_slice_in_dim(jnp.pad(item, (0, ff_pad)), block_start, block)
            for item in (gate_bias, up_bias)
        ]
    ).astype(f32)

    query_columns, keyvalue_columns = query_weight.shape[1], keyvalue_weight.shape[1]
    full_query = first[:, :query_columns]
    full_keyvalue = first[:, query_columns : query_columns + keyvalue_columns]
    vectors = first[:, query_columns + keyvalue_columns :].astype(f32)
    gain_one, full_obias, gain_two, full_dbias = (vectors[:, i] for i in range(4))
    norm_one_pull = jax.vjp(norm_scale, local_in, gain_one)[1]
    raw_rows = jnp.concatenate(in_order(plan.tensor, raw, raw_other), axis=0)
    normed = norm_scale(raw_rows.astype(f32), gain_one).astype(bf16)
    length = segments.shape[0]
    head_count = full_query.shape[1] // HD
    half_proj = jnp.dot(normed, full_keyvalue, preferred_element_type=f32)
    half_low = jnp.where(
        is_key, rotate(half_proj[:, None, :], cosine_table, sine_table, 1.0)[:, 0], half_proj
    ).astype(bf16)
    keyvalue = jnp.concatenate(in_order(plan.tensor, half_low, swap(half_low, plan.tensor)), axis=1)
    for bit in plan.ctx:
        keyvalue = jnp.concatenate([keyvalue, swap(keyvalue, bit)], axis=0)
        if bit == plan.y[-1]:
            keyvalue = ff_in.step(keyvalue)
    keyvalue, grad_local = tie(keyvalue, grad_local)
    all_keys = keyvalue[:, :HD]
    all_values = keyvalue[:, HD:]
    all_grads = lax.all_gather(
        grad_local, ("core", "near", "y", "tensor"), axis=0, tiled=True
    ).reshape(2, -1, width)
    query_proj = jnp.dot(normed, full_query, preferred_element_type=f32)
    queries = (
        rotate(query_proj.reshape(row_count, head_count, HD), cosine_table, sine_table, 1.0)
        * HD ** (-0.5)
    ).astype(bf16)
    queries = ff_in.step(queries)
    scores = jnp.einsum("qhd,kd->hqk", queries, all_keys, preferred_element_type=f32)
    scores = jnp.where(allowed[None], scores, -1e30)
    score_peak = jnp.max(scores, axis=-1, keepdims=True)
    exp_scores = jnp.exp(scores - score_peak)
    exp_total = jnp.sum(exp_scores, axis=-1, keepdims=True)
    probs = exp_scores / exp_total
    probs_low = probs.astype(bf16)
    context = jnp.einsum("hqk,kd->qhd", probs_low, all_values, preferred_element_type=f32)
    context = context.astype(bf16).reshape(row_count, head_count * HD)
    attended = jnp.einsum("rc,dc->rd", context, full_output, preferred_element_type=f32)
    attended = ff_in.step(attended)
    mixed = local_in + sum_rows(attended, plan) + full_obias
    mixed = ff_in.step(mixed)

    normed_two_local, norm_two_pull = jax.vjp(norm_scale, mixed, gain_two)
    journey = Journey(gather_tokens(normed_two_local.astype(bf16), plan))
    mixed = ff_in.step(journey.step(mixed))
    mixed = ff_in.finish(journey.step(mixed))
    mixed = journey.finish(mixed)
    normed_two = journey.result
    full_down, full_gate, full_up = ff_in.result
    full_pair = jnp.concatenate([full_gate, full_up], axis=1)
    core = lax.axis_index("core")
    grad_rows = [
        lax.dynamic_index_in_dim(all_grads, item, 0, keepdims=False) for item in (core, 1 - core)
    ]
    hidden, pair_grad, pair_bias_grad = [], [], 0.0
    for rows_two, rows_grad in zip(normed_two, grad_rows, strict=True):
        hidden_grad = jnp.dot(rows_grad, full_down, preferred_element_type=f32)
        pair_pre = jnp.dot(rows_two, full_pair, preferred_element_type=f32) + pair_bias
        gate_pre, up_pre = pair_pre[:, :block], pair_pre[:, block:]
        activated, gelu_pull = jax.vjp(partial(jax.nn.gelu, approximate=True), gate_pre)
        hidden.append((activated * up_pre).astype(bf16))
        pair_full = jnp.concatenate(
            [gelu_pull(hidden_grad * up_pre)[0], hidden_grad * activated], axis=1
        )
        pair_bias_grad = pair_bias_grad + jnp.sum(pair_full, axis=0)
        pair_grad.append(pair_full.astype(bf16))

    def rows_out(rows, weight):
        return jnp.einsum("rf,df->rd", rows, weight, preferred_element_type=f32).astype(bf16)

    def weight_out(lefts, rights):
        return sum(
            jnp.einsum("rd,rf->df", left, right, preferred_element_type=f32)
            for left, right in zip(lefts, rights, strict=True)
        ).astype(bf16)

    two_other = rows_out(pair_grad[1], full_pair)
    two_other, pair_grad = tie(two_other, pair_grad)
    two_own = rows_out(pair_grad[0], full_pair)
    two_sum = Journey(reduce_tokens(two_own, two_other, plan, token_count))
    hidden = two_sum.step(hidden)
    down_wgrad = weight_out(grad_rows, hidden)
    down_wgrad, pair_grad = two_sum.step((down_wgrad, pair_grad))
    down_sum = Journey(spread_out(down_wgrad, plan))
    out_other = rows_out(hidden[1], full_down)
    out_other, hidden, pair_grad = two_sum.step((out_other, hidden, pair_grad))
    out_own = rows_out(hidden[0], full_down)
    out_own, out_other, pair_grad = two_sum.finish((out_own, out_other, pair_grad))
    two_grad = two_sum.result

    grad_full = grad_local.astype(f32)
    dbias_part = jnp.sum(grad_full, axis=0)
    mixed_part, gain_two_part = norm_two_pull(two_grad)
    mixed_grad = grad_full + mixed_part
    obias_part = jnp.sum(mixed_grad, axis=0)
    mixed_low = mixed_grad.astype(bf16)
    mixed_other = swap(mixed_low, plan.tensor)
    out_other, mixed_low = tie(out_other, mixed_low)
    out_sum = Journey(reduce_tokens(out_own, out_other, plan, token_count))
    pair_grad, mixed_low = out_sum.step((pair_grad, mixed_low))
    gate_wgrad = weight_out(normed_two, [item[:, :block] for item in pair_grad])
    mixed_other, gate_wgrad = tie(mixed_other, gate_wgrad)
    gate_sum = Journey(spread_out(gate_wgrad, plan))
    attn_rows = jnp.concatenate(in_order(plan.tensor, mixed_low, mixed_other), axis=0)
    context_grad = jnp.dot(attn_rows, full_output, preferred_element_type=f32).astype(bf16)
    context_grad = context_grad.reshape(row_count, head_count, HD)
    context_grad, attn_rows = tie(context_grad, attn_rows)
    order = plan.ctx[::-1] + plan.near + plan.far[::-1]
    output_wgrad = jnp.einsum("rd,rc->dc", attn_rows, context, preferred_element_type=f32)
    context_grad, output_wgrad = tie(context_grad, output_wgrad.astype(bf16))
    output_sum = Journey(reduce_rows([output_wgrad], plan, [order]))
    probs_grad = jnp.einsum("qhd,kd->hqk", context_grad, all_values, preferred_element_type=f32)
    values_grad = jnp.einsum("hqk,qhd->kd", probs_low, context_grad, preferred_element_type=f32)
    prob_dot = jnp.sum(probs * probs_grad, axis=-1, keepdims=True)
    score_grad = (probs * (probs_grad - prob_dot)).astype(bf16)
    score_grad = output_sum.step(score_grad)
    keys_grad = jnp.einsum("hqk,qhd->kd", score_grad, queries, preferred_element_type=f32)
    stacked = jnp.concatenate([keys_grad, values_grad], axis=1)
    query_grad = jnp.einsum("hqk,kd->qhd", score_grad, all_keys, preferred_element_type=f32)
    query_proj_grad = rotate(query_grad * HD ** (-0.5), cosine_table, sine_table, -1.0)
    query_proj_grad = query_proj_grad.reshape(row_count, head_count * HD).astype(bf16)
    query_proj_grad = out_sum.step(query_proj_grad)
    query_wgrad = jnp.einsum("rd,rc->dc", normed, query_proj_grad, preferred_element_type=f32)
    query_wgrad = query_wgrad.astype(bf16)
    for bit in reversed(plan.ctx):
        half = stacked.shape[0] // 2
        other = swap(stacked[half:].astype(bf16), bit)
        if bit == plan.core:
            pair_grad, query_wgrad = tie(pair_grad, query_wgrad)
            up_wgrad = weight_out(normed_two, [item[:, block:] for item in pair_grad])
            other, up_wgrad, query_wgrad = out_sum.step((other, up_wgrad, query_wgrad))
            other, up_wgrad, query_wgrad = down_sum.step((other, up_wgrad, query_wgrad))
            up_sum = Journey(spread_out(up_wgrad, plan))
            query_sum = Journey(reduce_rows([query_wgrad], plan, [order]))
        stacked = stacked[:half] + other.astype(f32)
    mine, theirs = halves(stacked, plan.tensor, 1)
    half_grad = mine + swap(theirs.astype(bf16), plan.tensor).astype(f32)
    half_grad = query_sum.step(half_grad)
    half_grad = jnp.where(
        is_key, rotate(half_grad[:, None, :], cosine_table, sine_table, -1.0)[:, 0], half_grad
    ).astype(bf16)
    one_part = jnp.einsum(
        "rc,dc->rd", query_proj_grad, full_query, preferred_element_type=f32
    ) + jnp.einsum("rc,dc->rd", half_grad, full_keyvalue, preferred_element_type=f32)
    mine, theirs = halves(one_part, plan.tensor, 0)
    theirs, half_grad = tie(theirs.astype(bf16), half_grad)
    other = swap(theirs, plan.tensor)
    keyvalue_wgrad = jnp.einsum("rd,rc->dc", normed, half_grad, preferred_element_type=f32)
    keyvalue_wgrad = out_sum.finish(keyvalue_wgrad.astype(bf16))
    keyvalue_wgrad = output_sum.step(keyvalue_wgrad)
    keyvalue_wgrad = down_sum.step(keyvalue_wgrad)
    keyvalue_sum = Journey(reduce_rows([keyvalue_wgrad], plan, [order]))
    block_output = (mixed + out_sum.result + full_dbias).astype(bf16)
    block_output = gate_sum.step(block_output)
    other, block_output = tie(other, block_output)
    input_part, gain_one_part = norm_one_pull(mine + other.astype(f32))
    input_grad = mixed_grad + input_part

    for item in (
        keyvalue_sum,
        gate_sum,
        down_sum,
        output_sum,
        query_sum,
        up_sum,
        gate_sum,
        down_sum,
        up_sum,
        keyvalue_sum,
        output_sum,
        query_sum,
    ):
        input_grad = item.step(input_grad)

    small = jnp.stack([gain_one_part, gain_two_part, obias_part, dbias_part], axis=0)
    small = small.reshape(4, -1, shard_rows).transpose(1, 0, 2)
    small, pair_bias_grad, input_grad = tie(small, pair_bias_grad, input_grad)
    small = small + swap(small, plan.tensor)
    small_sum = Journey(reduce_rows([small.reshape(-1, shard_rows)], plan, [order], f32))
    ff_small = Journey(spread_small(pair_bias_grad.reshape(2, block), plan))
    journeys = [query_sum, gate_sum, up_sum, output_sum, small_sum, ff_small, keyvalue_sum, down_sum]
    while any(item.result is None for item in journeys):
        for item in journeys:
            if item.result is None:
                input_grad = item.step(input_grad)
    proj_out = output_sum.result[0]
    query_out = query_sum.result[0]
    keyvalue_out = keyvalue_sum.result[0]
    small = small_sum.result[0].reshape(4, shard_rows)
    ff_small = ff_small.result
    down_out, gate_out, up_out = (
        item.result[:, :ff_half].astype(f32) for item in (down_sum, gate_sum, up_sum)
    )
    return (
        block_output[None],
        input_grad[None],
        small[0],
        query_out,
        keyvalue_out,
        proj_out.T,
        small[2],
        small[1],
        gate_out,
        up_out,
        down_out.T,
        ff_small[0, :ff_half],
        ff_small[1, :ff_half],
        small[3],
    )


def solution(mesh):
    near = 2
    shape = (mesh.shape["dp"] // near, near, mesh.shape["ctx"] // 2, 2, mesh.shape["tensor"])
    names = DP + CTX + ("tensor",)
    mesh = Mesh(mesh.devices.reshape(shape), names)
    plan = Plan(dict(zip(names, shape, strict=True)))
    rows = P(DP, CTX + ("tensor",), None)
    vector = P(DP_CTX)
    wide = P(DP_CTX, "tensor")
    tall = P("tensor", DP_CTX)
    units = P("tensor")
    return jax.shard_map(
        partial(local, plan),
        mesh=mesh,
        in_specs=(
            rows,
            P(DP, CTX),
            rows,
            vector,
            wide,
            wide,
            tall,
            vector,
            vector,
            wide,
            wide,
            tall,
            units,
            units,
            vector,
        ),
        out_specs=(
            rows,
            rows,
            vector,
            wide,
            wide,
            tall,
            vector,
            vector,
            wide,
            wide,
            tall,
            units,
            units,
            vector,
        ),
        check_vma=False,
    )
```

```python
from functools import partial
import math

import jax
import jax.numpy as jnp
from jax import lax
from jax.experimental import pallas as pl
from jax.experimental.pallas import tpu as pltpu
from jax.sharding import Mesh
from jax.sharding import PartitionSpec as P

HD = 256
WINDOW = 2048
LANES = 128
GELU_SCALE = math.sqrt(2.0 / math.pi)
GELU_CUBE = 0.044715
DP = ("far", "near")
CTX = ("y", "core")
DP_CTX = DP + CTX
f32 = jnp.float32
bf16 = jnp.bfloat16


def norm_scale(vectors, scale_gain):
    return (
        vectors
        * lax.rsqrt(jnp.mean(vectors * vectors, axis=-1, keepdims=True) + 1e-06)
        * scale_gain
    )


def rotary_tables(positions, head_size):
    quarter = head_size // 4
    frequency = jnp.exp(jnp.arange(quarter, dtype=jnp.float32) * (-math.log(10000.0) / quarter))
    angles = positions.astype(jnp.float32)[:, None] * frequency[None, :]
    return (jnp.cos(angles), jnp.sin(angles))


def rotate(vectors, cosine_table, sine_table, direction):
    quarter = cosine_table.shape[-1]
    lead_part = vectors[..., :quarter]
    trail_part = vectors[..., quarter : 2 * quarter]
    cosine_wide = cosine_table[:, None, :]
    sine_wide = direction * sine_table[:, None, :]
    return jnp.concatenate(
        [
            lead_part * cosine_wide - trail_part * sine_wide,
            trail_part * cosine_wide + lead_part * sine_wide,
            vectors[..., 2 * quarter :],
        ],
        axis=-1,
    )


def bits_of(axis, size):
    masks = []
    while size > 1:
        size //= 2
        masks.append((axis, size))
    return masks


def swap(values, bit):
    axis, mask = bit
    return lax.ppermute(values, axis, [(i, i ^ mask) for i in range(lax.axis_size(axis))])


def digit(bit):
    axis, mask = bit
    return (lax.axis_index(axis) // mask) % 2


def in_order(bit, mine, other):
    one = digit(bit) == 1
    return jnp.where(one, other, mine), jnp.where(one, mine, other)


def halves(values, bit, axis):
    size = values.shape[axis] // 2
    own = digit(bit)
    return (
        lax.dynamic_slice_in_dim(values, own * size, size, axis),
        lax.dynamic_slice_in_dim(values, (1 - own) * size, size, axis),
    )


def tie(*groups):
    return lax.optimization_barrier(groups)


def finish_all(items, hold):
    while any(item.result is None for item in items):
        for item in items:
            if item.result is None:
                hold = item.step(hold)
    return hold


def tie_to(values, hold):
    return (values, None) if hold is None else tie(values, hold)


class Plan:
    def __init__(self, sizes):
        self.far = bits_of("far", sizes["far"])
        self.near = bits_of("near", sizes["near"])
        self.y = bits_of("y", sizes["y"])
        self.core = ("core", 1)
        self.tensor = ("tensor", 1)
        self.ctx = self.y + [self.core]
        self.rows = self.far + self.near + self.ctx
        self.links = [self.tensor] + self.y + self.near
        self.chip = self.near + self.y + [self.tensor]
        self.blocks = sizes["near"] * sizes["y"] * 2


class Journey:
    def __init__(self, steps):
        self.steps = steps
        self.result = None
        next(steps)

    def step(self, hold):
        try:
            return self.steps.send(hold)
        except StopIteration as end:
            self.result, hold = end.value
            return hold

    def finish(self, hold):
        while self.result is None:
            hold = self.step(hold)
        return hold


def repeat_in(arrays, plan, cuts, whole):
    hold = None
    for rows in arrays:
        size = rows.shape[0] // cuts
        pieces = []
        for start in range(0, rows.shape[0], size):
            piece = rows[start : start + size]
            if hold is not None:
                piece, hold = tie(piece, hold)
            for bit in reversed(plan.far):
                other = swap(piece, bit)
                hold = yield hold
                other, hold = tie_to(other, hold)
                piece = jnp.concatenate(in_order(bit, piece, other), axis=0)
            pieces.append(piece.reshape(-1, size, rows.shape[1]))
        whole.append(jnp.concatenate(pieces, axis=1).reshape(-1, rows.shape[1]))
    return whole, hold


def spread_back(grad, plan, bits):
    hold = None
    columns = grad.shape[-1]
    present = plan.near + plan.ctx
    grad = grad.reshape((2,) * len(present) + (-1, columns))
    for bit in bits:
        place = present.index(bit)
        present = present[:place] + present[place + 1 :]
        mine, theirs = halves(grad, bit, place)
        other = swap(jnp.squeeze(theirs, place), bit)
        hold = yield hold
        other, hold = tie_to(other, hold)
        grad = jnp.concatenate(in_order(bit, jnp.squeeze(mine, place), other), axis=-1)
    order = bits[::-1]
    if order != plan.near + plan.ctx:
        grad = grad.reshape((grad.shape[0],) + (2,) * len(bits) + (columns,))
        axes = [1 + order.index(bit) for bit in plan.near + plan.ctx]
        grad = grad.transpose([0] + axes + [len(bits) + 1]).reshape(grad.shape[0], -1)
    return grad, hold


def reduce_rows(grads, plan, orders, kind=bf16):
    hold = None
    states = [
        (grad.reshape((2,) * len(plan.rows) + (-1, grad.shape[-1])), list(plan.rows))
        for grad in grads
    ]
    for step in range(len(plan.rows)):
        kept, others = [], []
        for (grad, present), order in zip(states, orders, strict=True):
            place = present.index(order[step])
            mine, theirs = halves(grad, order[step], place)
            kept.append((jnp.squeeze(mine, place), present[:place] + present[place + 1 :]))
            others.append(jnp.squeeze(swap(theirs.astype(kind), order[step]), place))
        hold = yield hold
        others, hold = tie_to(others, hold)
        states = []
        for (mine, present), other in zip(kept, others, strict=True):
            grad = mine.astype(f32) + other.astype(f32)
            states.append((grad.astype(kind) if present else grad, present))
    return [grad for grad, _ in states], hold


def spread_small(part, plan):
    hold = None
    for bit in plan.far:
        other = swap(part, bit)
        hold = yield hold
        other, hold = tie_to(other, hold)
        part = part + other
    for bit in reversed(plan.near + plan.ctx):
        other = swap(part, bit)
        hold = yield hold
        other, hold = tie_to(other, hold)
        part = jnp.concatenate(in_order(bit, part, other), axis=1)
    return part, hold


def token_parts(count, plan):
    links = len(plan.links)
    step = 16
    units = count // step
    sizes = [(units + i) // links * step for i in range(links)]
    parts = []
    start = 0
    for i, size in enumerate(sizes):
        if size:
            parts.append((start, size, plan.links[i:] + plan.links[:i]))
            start += size
    return parts


def gather_tokens(local_rows, plan):
    hold = None
    parts = token_parts(local_rows.shape[0], plan)
    pieces = [(local_rows[start : start + size], []) for start, size, _ in parts]
    for step in range(len(plan.links)):
        bits = [order[step] for _, _, order in parts]
        others = [swap(piece, bit) for (piece, _), bit in zip(pieces, bits, strict=True)]
        hold = yield hold
        others, hold = tie_to(others, hold)
        grown = []
        for (piece, present), bit, other in zip(pieces, bits, others, strict=True):
            place = sum(1 for done in present if plan.chip.index(done) < plan.chip.index(bit))
            grown.append((jnp.stack(in_order(bit, piece, other), axis=place), present + [bit]))
        pieces = grown
    chip = jnp.concatenate([piece for piece, _ in pieces], axis=-2).reshape(
        -1, local_rows.shape[1]
    )
    return [chip, swap(chip, plan.core)], hold


def reduce_tokens(own, other, plan, count):
    got = swap(other, plan.core)
    hold = yield None
    got, hold = tie_to(got, hold)
    chip = (own.astype(f32) + got.astype(f32)).astype(bf16)
    chip = chip.reshape((2,) * len(plan.chip) + (count, -1))
    parts = token_parts(count, plan)
    pieces = [
        (lax.slice_in_dim(chip, start, start + size, axis=chip.ndim - 2), list(plan.chip))
        for start, size, _ in parts
    ]
    for step in reversed(range(len(plan.links))):
        kept, others = [], []
        for (piece, present), (_, _, order) in zip(pieces, parts, strict=True):
            place = present.index(order[step])
            mine, theirs = halves(piece, order[step], place)
            kept.append((jnp.squeeze(mine, place), present[:place] + present[place + 1 :]))
            others.append(swap(jnp.squeeze(theirs, place), order[step]))
        hold = yield hold
        others, hold = tie_to(others, hold)
        pieces = []
        for (mine, present), got in zip(kept, others, strict=True):
            piece = mine.astype(f32) + got.astype(f32)
            pieces.append((piece.astype(bf16) if present else piece, present))
    return jnp.concatenate([piece for piece, _ in pieces], axis=0), hold


def gather_rows(values_low, plan):
    return jnp.concatenate(in_order(plan.tensor, values_low, swap(values_low, plan.tensor)), axis=0)


def sum_rows(partial_rows, plan):
    mine, theirs = halves(partial_rows, plan.tensor, 0)
    return mine.astype(f32) + swap(theirs.astype(bf16), plan.tensor).astype(f32)


FREE = pl.CostEstimate(flops=0, bytes_accessed=0, transcendentals=0)
PARAMS = pltpu.CompilerParams(vmem_limit_bytes=48 * 2**20)
NN = (((1,), (0,)), ((), ()))
NT = (((1,), (1,)), ((), ()))
TN = (((0,), (0,)), ((), ()))


def dot(left, right, dims):
    return lax.dot_general(left, right, dims, preferred_element_type=f32)


def tile_of(size, most):
    return max(tile for tile in range(LANES, most + 1, LANES) if size % tile == 0)


def hidden_kernel(
    half_ref, rows_ref, grad_ref, gate_ref, up_ref, down_ref, bias_ref, hidden_ref, gate_grad_ref, up_grad_ref, sums_ref
):
    gate = dot(rows_ref[...], gate_ref[...], NN) + bias_ref[0:1]
    up = dot(rows_ref[...], up_ref[...], NN) + bias_ref[1:2]
    hidden_grad = dot(grad_ref[...], down_ref[...], NN)
    square = gate * gate
    bend = jnp.tanh(GELU_SCALE * gate * (1.0 + GELU_CUBE * square))
    half = 0.5 * (1.0 + bend)
    activated = gate * half
    slope = half + 0.5 * gate * (1.0 - bend * bend) * (
        GELU_SCALE * (1.0 + 3.0 * GELU_CUBE * square)
    )
    hidden_ref[...] = (activated * up).astype(bf16)
    gate_grad = hidden_grad * up * slope
    up_grad = hidden_grad * activated
    gate_grad_ref[...] = gate_grad.astype(bf16)
    up_grad_ref[...] = up_grad.astype(bf16)

    @pl.when(pl.program_id(0) == 0)
    def _():
        sums_ref[...] = jnp.zeros_like(sums_ref)

    sums_ref[0:1] += jnp.sum(gate_grad, axis=0, keepdims=True)
    sums_ref[1:2] += jnp.sum(up_grad, axis=0, keepdims=True)


def hidden_units(half, rows, grads, gate, up, down, bias):
    count, width = rows.shape
    block = gate.shape[1]
    tile = tile_of(count, 256)
    weight_spec = pl.BlockSpec((width, block), lambda i, half: (0, 0))
    unit_spec = pl.BlockSpec((tile, block), lambda i, half: (i, 0))
    pair_spec = pl.BlockSpec((2, block), lambda i, half: (0, 0))
    return pl.pallas_call(
        hidden_kernel,
        grid_spec=pltpu.PrefetchScalarGridSpec(
            num_scalar_prefetch=1,
            grid=(count // tile,),
            in_specs=[
                pl.BlockSpec((tile, width), lambda i, half: (i, 0)),
                pl.BlockSpec((tile, width), lambda i, half: (half[0] * (count // tile) + i, 0)),
                weight_spec,
                weight_spec,
                weight_spec,
                pair_spec,
            ],
            out_specs=[unit_spec, unit_spec, unit_spec, pair_spec],
        ),
        out_shape=[jax.ShapeDtypeStruct((count, block), bf16)] * 3
        + [jax.ShapeDtypeStruct((2, block), f32)],
        cost_estimate=FREE,
        compiler_params=PARAMS,
    )(half, rows, grads, gate, up, down, bias)


def rows_kernel(*refs):
    *pairs, out_ref = refs
    half = len(pairs) // 2
    out_ref[...] = sum(
        dot(left[...], right[...], NT)
        for left, right in zip(pairs[:half], pairs[half:], strict=True)
    ).astype(out_ref.dtype)


def rows_out(lefts, rights, kind=bf16, starts=None):
    count = lefts[0].shape[0]
    width = rights[0].shape[0]
    tile = tile_of(count, 256)
    depths = [item.shape[1] for item in lefts]
    places = [start // depth for start, depth in zip(starts or [0] * len(lefts), depths, strict=True)]
    return pl.pallas_call(
        rows_kernel,
        grid=(count // tile,),
        in_specs=[pl.BlockSpec((tile, depth), lambda i: (i, 0)) for depth in depths]
        + [
            pl.BlockSpec((width, depth), partial(lambda place, i: (0, place), place))
            for depth, place in zip(depths, places, strict=True)
        ],
        out_specs=pl.BlockSpec((tile, width), lambda i: (i, 0)),
        out_shape=jax.ShapeDtypeStruct((count, width), kind),
        cost_estimate=FREE,
        compiler_params=PARAMS,
    )(*lefts, *rights)


def turn(vectors, cosine, sine):
    lead = vectors[:, : HD // 2]
    lead = lead * cosine + pltpu.roll(lead, HD // 4, 1) * sine
    return jnp.concatenate([lead, vectors[:, HD // 2 :]], axis=1)


def attend_kernel(
    rows_ref, weight_ref, keys_ref, values_ref, allowed_ref, cosine_ref, sine_ref, queries_ref, context_ref, log_ref
):
    queries = dot(rows_ref[...], weight_ref[...], NN)
    queries = (turn(queries, cosine_ref[...], sine_ref[...]) * HD ** (-0.5)).astype(bf16)
    queries_ref[...] = queries
    scores = jnp.where(allowed_ref[...] > 0, dot(queries, keys_ref[...], NT), -1e30)
    peak = jnp.max(scores, axis=1, keepdims=True)
    powers = jnp.exp(scores - peak)
    total = jnp.sum(powers, axis=1, keepdims=True)
    probs_low = (powers / total).astype(bf16)
    context_ref[...] = dot(probs_low, values_ref[...], NN).astype(bf16)
    log_ref[...] = jnp.broadcast_to(peak + jnp.log(total), log_ref.shape)


def attend(rows, weights, keyvalue, allowed, cosine, sine, head_count):
    count, width = rows.shape
    length = keyvalue.shape[0]
    head = pl.BlockSpec((count, HD), lambda h: (0, h))
    table = pl.BlockSpec((count, HD // 2), lambda h: (0, 0))
    return pl.pallas_call(
        attend_kernel,
        grid=(head_count,),
        in_specs=[
            pl.BlockSpec((count, width), lambda h: (0, 0)),
            pl.BlockSpec((width, HD), lambda h: (0, h)),
            pl.BlockSpec((length, HD), lambda h: (0, 0)),
            pl.BlockSpec((length, HD), lambda h: (0, 1)),
            pl.BlockSpec((count, length), lambda h: (0, 0)),
            table,
            table,
        ],
        out_specs=[head, head, pl.BlockSpec((count, LANES), lambda h: (0, h))],
        out_shape=[jax.ShapeDtypeStruct((count, head_count * HD), bf16)] * 2
        + [jax.ShapeDtypeStruct((count, head_count * LANES), f32)],
        cost_estimate=FREE,
        compiler_params=PARAMS,
    )(rows, weights, keyvalue, keyvalue, allowed, cosine, sine)


def attend_back_kernel(
    rows_ref, weight_ref, queries_ref, log_ref, keys_ref, values_ref, allowed_ref, cosine_ref, sine_ref, query_ref, sums_ref
):
    context_grad = dot(rows_ref[...], weight_ref[...], NN).astype(bf16)
    queries, keys = queries_ref[...], keys_ref[...]
    scores = jnp.where(allowed_ref[...] > 0, dot(queries, keys, NT), -1e30)
    probs = jnp.exp(scores - log_ref[:, :1])
    probs_grad = dot(context_grad, values_ref[...], NT)
    prob_dot = jnp.sum(probs * probs_grad, axis=1, keepdims=True)
    score_grad = (probs * (probs_grad - prob_dot)).astype(bf16)
    query_grad = dot(score_grad, keys, NN) * HD ** (-0.5)
    query_ref[...] = turn(query_grad, cosine_ref[...], -sine_ref[...]).astype(bf16)

    @pl.when(pl.program_id(0) == 0)
    def _():
        sums_ref[...] = jnp.zeros_like(sums_ref)

    sums_ref[:, :HD] += dot(score_grad, queries, TN)
    sums_ref[:, HD:] += dot(probs.astype(bf16), context_grad, TN)


def attend_back(rows, weights, queries, logs, keyvalue, allowed, cosine, sine):
    count, width = rows.shape
    length = keyvalue.shape[0]
    head = pl.BlockSpec((count, HD), lambda h: (0, h))
    table = pl.BlockSpec((count, HD // 2), lambda h: (0, 0))
    return pl.pallas_call(
        attend_back_kernel,
        grid=(queries.shape[1] // HD,),
        in_specs=[
            pl.BlockSpec((count, width), lambda h: (0, 0)),
            pl.BlockSpec((width, HD), lambda h: (0, h)),
            head,
            pl.BlockSpec((count, LANES), lambda h: (0, h)),
            pl.BlockSpec((length, HD), lambda h: (0, 0)),
            pl.BlockSpec((length, HD), lambda h: (0, 1)),
            pl.BlockSpec((count, length), lambda h: (0, 0)),
            table,
            table,
        ],
        out_specs=[head, pl.BlockSpec((length, 2 * HD), lambda h: (0, 0))],
        out_shape=[
            jax.ShapeDtypeStruct(queries.shape, bf16),
            jax.ShapeDtypeStruct((length, 2 * HD), f32),
        ],
        cost_estimate=FREE,
        compiler_params=PARAMS,
    )(rows, weights, queries, logs, keyvalue, keyvalue, allowed, cosine, sine)


def weight_kernel(groups, half_ref, *refs):
    *pairs, out_ref = refs
    start = 0
    for lefts, rights in groups:
        size = pairs[rights[0]].shape[1]
        out_ref[:, start : start + size] = sum(
            dot(pairs[left][...], pairs[right][...], TN)
            for left, right in zip(lefts, rights, strict=True)
        ).astype(out_ref.dtype)
        start += size


def weight_out(half, *products):
    arrays, specs, groups, columns = [], [], [], 0
    count = products[0][1][0].shape[0]
    width = products[0][0][0].shape[1]
    tile = tile_of(width, 512)
    straight = pl.BlockSpec((count, tile), lambda i, half: (0, i))
    first = pl.BlockSpec((count, tile), lambda i, half: (half[0], i))
    second = pl.BlockSpec((count, tile), lambda i, half: (1 - half[0], i))
    known = {}
    for lefts, rights in products:
        halved = len(lefts) < len(rights)
        group = []
        for items, item_specs in (
            (lefts * 2 if halved else lefts, [first, second] if halved else [straight] * len(lefts)),
            (
                rights,
                [pl.BlockSpec((count, item.shape[1]), lambda i, half: (0, 0)) for item in rights],
            ),
        ):
            places = []
            for item, spec in zip(items, item_specs, strict=True):
                key = (id(item), id(spec) if halved else 0)
                if key not in known:
                    known[key] = len(arrays)
                    arrays.append(item)
                    specs.append(spec)
                places.append(known[key])
            group.append(places)
        groups.append(group)
        columns += rights[0].shape[1]
    return pl.pallas_call(
        partial(weight_kernel, groups),
        grid_spec=pltpu.PrefetchScalarGridSpec(
            num_scalar_prefetch=1,
            grid=(width // tile,),
            in_specs=specs,
            out_specs=pl.BlockSpec((tile, columns), lambda i, half: (i, 0)),
        ),
        out_shape=jax.ShapeDtypeStruct((width, columns), bf16),
        cost_estimate=FREE,
        compiler_params=PARAMS,
    )(half, *arrays)


def local(
    plan,
    block_input,
    segment_ids,
    output_grad,
    attention_gain,
    query_weight,
    keyvalue_weight,
    output_weight,
    output_bias,
    channel_gain,
    gate_weight,
    up_weight,
    down_weight,
    gate_bias,
    up_bias,
    down_bias,
):
    local_in = block_input[0].astype(f32)
    grad_local = output_grad[0]
    is_key = lax.axis_index("tensor") == 0
    ctx_index = lax.axis_index("y") * 2 + lax.axis_index("core")
    shard_rows = attention_gain.shape[0]
    token_count, width = local_in.shape
    ff_half = gate_bias.shape[0]
    blocks = plan.blocks
    block = -(-ff_half // (blocks * LANES)) * LANES
    ff_pad = blocks * block - ff_half

    segments = segment_ids[0]
    row_count = segments.shape[0]
    offsets = [0]
    for axis, mask in plan.ctx:
        segments = jnp.concatenate([segments, swap(segments, (axis, mask))])
        offsets = offsets + [item ^ (mask * 2 if axis == "y" else mask) for item in offsets]
    piece_index = jnp.arange(row_count, dtype=jnp.int32)
    key_index = jnp.concatenate([(ctx_index ^ item) * row_count + piece_index for item in offsets])
    own_segments = segments[:row_count]
    query_index = key_index[:row_count]
    earlier = jnp.sum((segments[None, :] < own_segments[:, None]).astype(jnp.int32), axis=1)
    cosine_table, sine_table = rotary_tables(query_index - earlier, HD)
    allowed = (
        (own_segments[:, None] == segments[None, :])
        & (key_index[None, :] <= query_index[:, None])
        & (query_index[:, None] - key_index[None, :] < WINDOW)
    ).astype(f32)
    cosine_both = jnp.concatenate([cosine_table, cosine_table], axis=1)
    sine_both = jnp.concatenate([-sine_table, sine_table], axis=1)

    def by_block(item):
        return lax.all_to_all(
            jnp.pad(item, ((0, 0), (0, ff_pad))),
            ("near",) + CTX,
            split_axis=1,
            concat_axis=0,
            tiled=True,
        )

    raw = block_input[0]
    raw_other = swap(raw, plan.tensor)
    down_rows, gate_rows, up_rows = (
        by_block(item) for item in (down_weight.T, gate_weight, up_weight)
    )

    vectors = jnp.stack([attention_gain, output_bias, channel_gain, down_bias], axis=1)
    vectors = jnp.pad(vectors, ((0, 0), (0, LANES - 4)))
    first = lax.all_gather(
        jnp.concatenate([query_weight, keyvalue_weight, vectors], axis=1),
        DP_CTX,
        axis=0,
        tiled=True,
    )
    full_output = lax.all_gather(output_weight.T, DP_CTX, axis=0, tiled=True)

    first, raw_other, *ff_rows = tie(first, raw_other, down_rows, gate_rows, up_rows)
    full_ff = []
    ff_in = Journey(repeat_in(ff_rows, plan, 2, full_ff))
    block_start = (lax.axis_index("near") * (blocks // 2) + ctx_index) * block
    pair_bias = jnp.stack(
        [
            lax.dynamic_slice_in_dim(jnp.pad(item, (0, ff_pad)), block_start, block)
            for item in (gate_bias, up_bias)
        ]
    ).astype(f32)

    query_columns, keyvalue_columns = query_weight.shape[1], keyvalue_weight.shape[1]
    full_keyvalue = first[:, query_columns : query_columns + keyvalue_columns]
    vectors = first[:, query_columns + keyvalue_columns :].astype(f32)
    gain_one, full_obias, gain_two, full_dbias = (vectors[:, i] for i in range(4))
    norm_one_pull = jax.vjp(norm_scale, local_in, gain_one)[1]
    raw_rows = jnp.concatenate(in_order(plan.tensor, raw, raw_other), axis=0)
    normed = norm_scale(raw_rows.astype(f32), gain_one).astype(bf16)
    head_count = query_columns // HD
    half_proj = jnp.dot(normed, full_keyvalue, preferred_element_type=f32)
    half_low = jnp.where(
        is_key, rotate(half_proj[:, None, :], cosine_table, sine_table, 1.0)[:, 0], half_proj
    ).astype(bf16)
    keyvalue = jnp.concatenate(in_order(plan.tensor, half_low, swap(half_low, plan.tensor)), axis=1)
    for bit in plan.ctx:
        keyvalue = jnp.concatenate([keyvalue, swap(keyvalue, bit)], axis=0)
        if bit == plan.y[-1]:
            keyvalue = ff_in.step(keyvalue)
    keyvalue, grad_local = tie(keyvalue, grad_local)
    all_grads = lax.all_gather(
        grad_local, ("core", "near", "y", "tensor"), axis=0, tiled=True
    )
    keyvalue = ff_in.step(keyvalue)
    queries, context, logs = attend(
        normed, first, keyvalue, allowed, cosine_both, sine_both, head_count
    )
    attended = rows_out([context], [full_output], f32)
    attended = ff_in.step(attended)
    mixed = local_in + sum_rows(attended, plan) + full_obias
    mixed = ff_in.step(mixed)

    normed_two_local, norm_two_pull = jax.vjp(norm_scale, mixed, gain_two)
    journey = Journey(gather_tokens(normed_two_local.astype(bf16), plan))
    mixed = ff_in.step(journey.step(mixed))
    mixed = ff_in.finish(journey.step(mixed))
    mixed, full_ff = tie(mixed, full_ff)
    mixed = journey.finish(mixed)
    normed_two = journey.result
    full_down, full_gate, full_up = full_ff
    core = lax.axis_index("core")
    own_half, other_half = (jnp.full((1,), item, jnp.int32) for item in (core, 1 - core))
    weights = (full_gate, full_up, full_down, pair_bias)
    own_part = hidden_units(own_half, normed_two[0], all_grads, *weights)
    normed_two[1], own_part = tie(normed_two[1], own_part)
    parts = [own_part, hidden_units(other_half, normed_two[1], all_grads, *weights)]
    hidden, gate_grad, up_grad, bias_sums = (list(item) for item in zip(*parts, strict=True))
    pair_weights = [full_gate, full_up]
    two_other = rows_out([gate_grad[1], up_grad[1]], pair_weights)
    ff_small = Journey(spread_small(sum(bias_sums), plan))
    two_other, gate_grad, up_grad = tie(two_other, gate_grad, up_grad)
    two_own = rows_out([gate_grad[0], up_grad[0]], pair_weights)
    two_own = ff_small.step(two_own)
    two_sum = Journey(reduce_tokens(two_own, two_other, plan, token_count))
    gate_grad, up_grad, hidden = two_sum.step((gate_grad, up_grad, hidden))
    ff_wgrad = weight_out(
        own_half, ([all_grads], hidden), (normed_two, gate_grad), (normed_two, up_grad)
    )
    ff_wgrad, hidden = ff_small.step(two_sum.step((ff_wgrad, hidden)))
    ff_sum = lax.psum_scatter(ff_wgrad, "far", scatter_dimension=0, tiled=True)
    hidden = ff_small.step(two_sum.step(hidden))
    hidden = two_sum.finish(hidden)
    two_grad = two_sum.result

    grad_full = grad_local.astype(f32)
    dbias_part = jnp.sum(grad_full, axis=0)
    mixed_part, gain_two_part = norm_two_pull(two_grad)
    mixed_grad = grad_full + mixed_part
    obias_part = jnp.sum(mixed_grad, axis=0)
    mixed_low = mixed_grad.astype(bf16)
    mixed_other = swap(mixed_low, plan.tensor)
    hidden, mixed_low = tie(hidden, mixed_low)
    out_other = rows_out([hidden[1]], [full_down])
    out_other, hidden = tie(out_other, hidden)
    out_own = rows_out([hidden[0]], [full_down])
    out_sum = Journey(reduce_tokens(out_own, out_other, plan, token_count))
    mixed_other, out_own = tie(mixed_other, out_own)
    attn_rows = jnp.concatenate(in_order(plan.tensor, mixed_low, mixed_other), axis=0)
    order_one = plan.ctx[::-1] + plan.near + plan.far[::-1]
    order_two = [plan.core] + plan.near + plan.y[::-1] + plan.far[::-1]
    attn_rows = ff_small.finish(out_sum.step(attn_rows))
    query_proj_grad, stacked = attend_back(
        attn_rows, full_output, queries, logs, keyvalue, allowed, cosine_both, sine_both
    )
    stacked, query_proj_grad, attn_rows = tie(stacked, query_proj_grad, attn_rows)
    query_wgrad = weight_out(own_half, ([normed], [query_proj_grad]))
    for bit in reversed(plan.ctx):
        half = stacked.shape[0] // 2
        other = swap(stacked[half:].astype(bf16), bit)
        if bit == plan.core:
            other, query_wgrad, attn_rows = tie(other, query_wgrad, attn_rows)
            query_sum = Journey(reduce_rows([query_wgrad], plan, [order_one]))
            output_wgrad = weight_out(own_half, ([attn_rows], [context]))
        elif bit == plan.y[-1]:
            other, output_wgrad = query_sum.step(out_sum.step((other, output_wgrad)))
        stacked = stacked[:half] + other.astype(f32)
    mine, theirs = halves(stacked, plan.tensor, 1)
    half_grad = mine + swap(theirs.astype(bf16), plan.tensor).astype(f32)
    half_grad = jnp.where(
        is_key, rotate(half_grad[:, None, :], cosine_table, sine_table, -1.0)[:, 0], half_grad
    ).astype(bf16)
    one_part = rows_out([query_proj_grad, half_grad], [first, first], f32, [0, query_columns])
    mine, theirs = halves(one_part, plan.tensor, 0)
    theirs, half_grad, output_wgrad = tie(theirs.astype(bf16), half_grad, output_wgrad)
    other = swap(theirs, plan.tensor)
    keyvalue_wgrad = weight_out(own_half, ([normed], [half_grad]))
    other, keyvalue_wgrad, output_wgrad = out_sum.step((other, keyvalue_wgrad, output_wgrad))
    input_part, gain_one_part = norm_one_pull(mine + other.astype(f32))
    input_grad = mixed_grad + input_part
    input_grad, output_wgrad, keyvalue_wgrad = out_sum.finish(
        (input_grad, output_wgrad, keyvalue_wgrad)
    )
    block_output = (mixed + out_sum.result + full_dbias).astype(bf16)

    small = jnp.stack([gain_one_part, gain_two_part, obias_part, dbias_part], axis=0)
    small = small.reshape(4, -1, shard_rows).transpose(1, 0, 2)
    small = small + swap(small, plan.tensor)
    small_sum = Journey(reduce_rows([small.reshape(-1, shard_rows)], plan, [order_one], f32))
    keyvalue_sum = Journey(reduce_rows([keyvalue_wgrad], plan, [order_one]))
    for item in (small_sum, keyvalue_sum, query_sum):
        input_grad = item.step(input_grad)
    output_wgrad, input_grad = tie(output_wgrad, input_grad)
    output_sum = Journey(reduce_rows([output_wgrad], plan, [order_one]))
    for item in (small_sum, keyvalue_sum, output_sum):
        input_grad = item.step(input_grad)
    ff_sum, input_grad = tie(ff_sum, input_grad)
    y_first = [plan.core] + plan.y[::-1] + plan.near[::-1]
    near_first = [plan.core] + plan.near[::-1] + plan.y[::-1]
    backs = [
        Journey(spread_back(ff_sum[:, i * block : (i + 1) * block], plan, bits))
        for i, bits in enumerate((y_first, near_first, y_first))
    ]
    for item in (small_sum, keyvalue_sum, query_sum, *backs, small_sum, keyvalue_sum):
        if item.result is None:
            input_grad = item.step(input_grad)
    input_grad = finish_all(
        [output_sum, *backs, keyvalue_sum, small_sum, query_sum], input_grad
    )
    proj_out = output_sum.result[0]
    query_out = query_sum.result[0]
    keyvalue_out = keyvalue_sum.result[0]
    small = small_sum.result[0].reshape(4, shard_rows)
    ff_small = ff_small.result
    down_out, gate_out, up_out = (item.result[:, :ff_half].astype(f32) for item in backs)
    return (
        block_output[None],
        input_grad[None],
        small[0],
        query_out,
        keyvalue_out,
        proj_out.T,
        small[2],
        small[1],
        gate_out,
        up_out,
        down_out.T,
        ff_small[0, :ff_half],
        ff_small[1, :ff_half],
        small[3],
    )


def solution(mesh):
    near = 2
    shape = (mesh.shape["dp"] // near, near, mesh.shape["ctx"] // 2, 2, mesh.shape["tensor"])
    names = DP + CTX + ("tensor",)
    mesh = Mesh(mesh.devices.reshape(shape), names)
    plan = Plan(dict(zip(names, shape, strict=True)))
    rows = P(DP, CTX + ("tensor",), None)
    vector = P(DP_CTX)
    wide = P(DP_CTX, "tensor")
    tall = P("tensor", DP_CTX)
    units = P("tensor")
    return jax.shard_map(
        partial(local, plan),
        mesh=mesh,
        in_specs=(
            rows,
            P(DP, CTX),
            rows,
            vector,
            wide,
            wide,
            tall,
            vector,
            vector,
            wide,
            wide,
            tall,
            units,
            units,
            vector,
        ),
        out_specs=(
            rows,
            rows,
            vector,
            wide,
            wide,
            tall,
            vector,
            vector,
            wide,
            wide,
            tall,
            units,
            units,
            vector,
        ),
        check_vma=False,
    )
```

```python
from functools import partial
import math

import jax
import jax.numpy as jnp
from jax import lax
from jax.experimental import pallas as pl
from jax.experimental.pallas import tpu as pltpu
from jax.sharding import Mesh
from jax.sharding import PartitionSpec as P

HD = 256
WINDOW = 2048
LANES = 128
GELU_SCALE = math.sqrt(2.0 / math.pi)
GELU_CUBE = 0.044715
DP = ("far", "near")
CTX = ("y", "core")
DP_CTX = DP + CTX
f32 = jnp.float32
bf16 = jnp.bfloat16


def norm_scale(vectors, scale_gain):
    return (
        vectors
        * lax.rsqrt(jnp.mean(vectors * vectors, axis=-1, keepdims=True) + 1e-06)
        * scale_gain
    )


def rotary_tables(positions, head_size):
    quarter = head_size // 4
    frequency = jnp.exp(jnp.arange(quarter, dtype=jnp.float32) * (-math.log(10000.0) / quarter))
    angles = positions.astype(jnp.float32)[:, None] * frequency[None, :]
    return (jnp.cos(angles), jnp.sin(angles))


def rotate(vectors, cosine_table, sine_table, direction):
    quarter = cosine_table.shape[-1]
    lead_part = vectors[..., :quarter]
    trail_part = vectors[..., quarter : 2 * quarter]
    cosine_wide = cosine_table[:, None, :]
    sine_wide = direction * sine_table[:, None, :]
    return jnp.concatenate(
        [
            lead_part * cosine_wide - trail_part * sine_wide,
            trail_part * cosine_wide + lead_part * sine_wide,
            vectors[..., 2 * quarter :],
        ],
        axis=-1,
    )


def bits_of(axis, size):
    masks = []
    while size > 1:
        size //= 2
        masks.append((axis, size))
    return masks


def swap(values, bit):
    axis, mask = bit
    return lax.ppermute(values, axis, [(i, i ^ mask) for i in range(lax.axis_size(axis))])


def digit(bit):
    axis, mask = bit
    return (lax.axis_index(axis) // mask) % 2


def in_order(bit, mine, other):
    one = digit(bit) == 1
    return jnp.where(one, other, mine), jnp.where(one, mine, other)


def halves(values, bit, axis):
    size = values.shape[axis] // 2
    own = digit(bit)
    return (
        lax.dynamic_slice_in_dim(values, own * size, size, axis),
        lax.dynamic_slice_in_dim(values, (1 - own) * size, size, axis),
    )


def tie(*groups):
    return lax.optimization_barrier(groups)


def finish_all(items, hold):
    while any(item.result is None for item in items):
        for item in items:
            if item.result is None:
                hold = item.step(hold)
    return hold


def tie_to(values, hold):
    return (values, None) if hold is None else tie(values, hold)


class Plan:
    def __init__(self, sizes):
        self.far = bits_of("far", sizes["far"])
        self.near = bits_of("near", sizes["near"])
        self.y = bits_of("y", sizes["y"])
        self.core = ("core", 1)
        self.tensor = ("tensor", 1)
        self.ctx = self.y + [self.core]
        self.rows = self.far + self.near + self.ctx
        self.links = [self.tensor] + self.y + self.near
        self.chip = self.near + self.y + [self.tensor]
        self.blocks = sizes["near"] * sizes["y"] * 2


class Journey:
    def __init__(self, steps):
        self.steps = steps
        self.result = None
        next(steps)

    def step(self, hold):
        try:
            return self.steps.send(hold)
        except StopIteration as end:
            self.result, hold = end.value
            return hold

    def finish(self, hold):
        while self.result is None:
            hold = self.step(hold)
        return hold


def repeat_in(arrays, plan, cuts, whole):
    hold = None
    for rows in arrays:
        size = rows.shape[0] // cuts
        pieces = []
        for start in range(0, rows.shape[0], size):
            piece = rows[start : start + size]
            if hold is not None:
                piece, hold = tie(piece, hold)
            for bit in reversed(plan.far):
                other = swap(piece, bit)
                hold = yield hold
                other, hold = tie_to(other, hold)
                piece = jnp.concatenate(in_order(bit, piece, other), axis=0)
            pieces.append(piece.reshape(-1, size, rows.shape[1]))
        whole.append(jnp.concatenate(pieces, axis=1).reshape(-1, rows.shape[1]))
    return whole, hold


def spread_back(grad, plan, bits):
    hold = None
    columns = grad.shape[-1]
    present = plan.near + plan.ctx
    grad = grad.reshape((2,) * len(present) + (-1, columns))
    for bit in bits:
        place = present.index(bit)
        present = present[:place] + present[place + 1 :]
        mine, theirs = halves(grad, bit, place)
        other = swap(jnp.squeeze(theirs, place), bit)
        hold = yield hold
        other, hold = tie_to(other, hold)
        grad = jnp.concatenate(in_order(bit, jnp.squeeze(mine, place), other), axis=-1)
    order = bits[::-1]
    if order != plan.near + plan.ctx:
        grad = grad.reshape((grad.shape[0],) + (2,) * len(bits) + (columns,))
        axes = [1 + order.index(bit) for bit in plan.near + plan.ctx]
        grad = grad.transpose([0] + axes + [len(bits) + 1]).reshape(grad.shape[0], -1)
    return grad, hold


def reduce_rows(grads, plan, orders, kind=bf16):
    hold = None
    states = [
        (grad.reshape((2,) * len(plan.rows) + (-1, grad.shape[-1])), list(plan.rows))
        for grad in grads
    ]
    for step in range(len(plan.rows)):
        kept, others = [], []
        for (grad, present), order in zip(states, orders, strict=True):
            place = present.index(order[step])
            mine, theirs = halves(grad, order[step], place)
            kept.append((jnp.squeeze(mine, place), present[:place] + present[place + 1 :]))
            others.append(jnp.squeeze(swap(theirs.astype(kind), order[step]), place))
        hold = yield hold
        others, hold = tie_to(others, hold)
        states = []
        for (mine, present), other in zip(kept, others, strict=True):
            grad = mine.astype(f32) + other.astype(f32)
            states.append((grad.astype(kind) if present else grad, present))
    return [grad for grad, _ in states], hold


def spread_small(part, plan):
    hold = None
    for bit in plan.far:
        other = swap(part, bit)
        hold = yield hold
        other, hold = tie_to(other, hold)
        part = part + other
    for bit in reversed(plan.near + plan.ctx):
        other = swap(part, bit)
        hold = yield hold
        other, hold = tie_to(other, hold)
        part = jnp.concatenate(in_order(bit, part, other), axis=1)
    return part, hold


def token_parts(count, plan):
    links = len(plan.links)
    step = 16
    units = count // step
    sizes = [(units + i) // links * step for i in range(links)]
    parts = []
    start = 0
    for i, size in enumerate(sizes):
        if size:
            parts.append((start, size, plan.links[i:] + plan.links[:i]))
            start += size
    return parts


def gather_tokens(local_rows, plan):
    hold = None
    parts = token_parts(local_rows.shape[0], plan)
    pieces = [(local_rows[start : start + size], []) for start, size, _ in parts]
    for step in range(len(plan.links)):
        bits = [order[step] for _, _, order in parts]
        others = [swap(piece, bit) for (piece, _), bit in zip(pieces, bits, strict=True)]
        hold = yield hold
        others, hold = tie_to(others, hold)
        grown = []
        for (piece, present), bit, other in zip(pieces, bits, others, strict=True):
            place = sum(1 for done in present if plan.chip.index(done) < plan.chip.index(bit))
            grown.append((jnp.stack(in_order(bit, piece, other), axis=place), present + [bit]))
        pieces = grown
    chip = jnp.concatenate([piece for piece, _ in pieces], axis=-2).reshape(
        -1, local_rows.shape[1]
    )
    return [chip, swap(chip, plan.core)], hold


def reduce_tokens(own, other, plan, count):
    got = swap(other, plan.core)
    hold = yield None
    got, hold = tie_to(got, hold)
    chip = (own.astype(f32) + got.astype(f32)).astype(bf16)
    chip = chip.reshape((2,) * len(plan.chip) + (count, -1))
    parts = token_parts(count, plan)
    pieces = [
        (lax.slice_in_dim(chip, start, start + size, axis=chip.ndim - 2), list(plan.chip))
        for start, size, _ in parts
    ]
    for step in reversed(range(len(plan.links))):
        kept, others = [], []
        for (piece, present), (_, _, order) in zip(pieces, parts, strict=True):
            place = present.index(order[step])
            mine, theirs = halves(piece, order[step], place)
            kept.append((jnp.squeeze(mine, place), present[:place] + present[place + 1 :]))
            others.append(swap(jnp.squeeze(theirs, place), order[step]))
        hold = yield hold
        others, hold = tie_to(others, hold)
        pieces = []
        for (mine, present), got in zip(kept, others, strict=True):
            piece = mine.astype(f32) + got.astype(f32)
            pieces.append((piece.astype(bf16) if present else piece, present))
    return jnp.concatenate([piece for piece, _ in pieces], axis=0), hold


def gather_rows(values_low, plan):
    return jnp.concatenate(in_order(plan.tensor, values_low, swap(values_low, plan.tensor)), axis=0)


def sum_rows(partial_rows, plan):
    mine, theirs = halves(partial_rows, plan.tensor, 0)
    return mine.astype(f32) + swap(theirs.astype(bf16), plan.tensor).astype(f32)


FREE = pl.CostEstimate(flops=0, bytes_accessed=0, transcendentals=0)
PARAMS = pltpu.CompilerParams(vmem_limit_bytes=48 * 2**20)
NN = (((1,), (0,)), ((), ()))
NT = (((1,), (1,)), ((), ()))
TN = (((0,), (0,)), ((), ()))


def dot(left, right, dims):
    return lax.dot_general(left, right, dims, preferred_element_type=f32)


def tile_of(size, most):
    return max(tile for tile in range(LANES, most + 1, LANES) if size % tile == 0)


def hidden_kernel(
    half_ref, rows_ref, grad_ref, gate_ref, up_ref, down_ref, bias_ref, hidden_ref, gate_grad_ref, up_grad_ref, sums_ref
):
    gate = dot(rows_ref[...], gate_ref[...], NN) + bias_ref[0:1]
    up = dot(rows_ref[...], up_ref[...], NN) + bias_ref[1:2]
    hidden_grad = dot(grad_ref[...], down_ref[...], NN)
    square = gate * gate
    bend = jnp.tanh(GELU_SCALE * gate * (1.0 + GELU_CUBE * square))
    half = 0.5 * (1.0 + bend)
    activated = gate * half
    slope = half + 0.5 * gate * (1.0 - bend * bend) * (
        GELU_SCALE * (1.0 + 3.0 * GELU_CUBE * square)
    )
    hidden_ref[...] = (activated * up).astype(bf16)
    gate_grad = hidden_grad * up * slope
    up_grad = hidden_grad * activated
    gate_grad_ref[...] = gate_grad.astype(bf16)
    up_grad_ref[...] = up_grad.astype(bf16)

    @pl.when(pl.program_id(0) == 0)
    def _():
        sums_ref[...] = jnp.zeros_like(sums_ref)

    sums_ref[0:1] += jnp.sum(gate_grad, axis=0, keepdims=True)
    sums_ref[1:2] += jnp.sum(up_grad, axis=0, keepdims=True)


def hidden_units(half, rows, grads, gate, up, down, bias):
    count, width = rows.shape
    block = gate.shape[1]
    tile = tile_of(count, 256)
    weight_spec = pl.BlockSpec((width, block), lambda i, half: (0, 0))
    unit_spec = pl.BlockSpec((tile, block), lambda i, half: (i, 0))
    pair_spec = pl.BlockSpec((2, block), lambda i, half: (0, 0))
    return pl.pallas_call(
        hidden_kernel,
        grid_spec=pltpu.PrefetchScalarGridSpec(
            num_scalar_prefetch=1,
            grid=(count // tile,),
            in_specs=[
                pl.BlockSpec((tile, width), lambda i, half: (i, 0)),
                pl.BlockSpec((tile, width), lambda i, half: (half[0] * (count // tile) + i, 0)),
                weight_spec,
                weight_spec,
                weight_spec,
                pair_spec,
            ],
            out_specs=[unit_spec, unit_spec, unit_spec, pair_spec],
        ),
        out_shape=[jax.ShapeDtypeStruct((count, block), bf16)] * 3
        + [jax.ShapeDtypeStruct((2, block), f32)],
        cost_estimate=FREE,
        compiler_params=PARAMS,
    )(half, rows, grads, gate, up, down, bias)


def rows_kernel(*refs):
    *pairs, out_ref = refs
    half = len(pairs) // 2
    out_ref[...] = sum(
        dot(left[...], right[...], NT)
        for left, right in zip(pairs[:half], pairs[half:], strict=True)
    ).astype(out_ref.dtype)


def rows_out(lefts, rights, kind=bf16, starts=None):
    count = lefts[0].shape[0]
    width = rights[0].shape[0]
    tile = tile_of(count, 256)
    depths = [item.shape[1] for item in lefts]
    places = [start // depth for start, depth in zip(starts or [0] * len(lefts), depths, strict=True)]
    return pl.pallas_call(
        rows_kernel,
        grid=(count // tile,),
        in_specs=[pl.BlockSpec((tile, depth), lambda i: (i, 0)) for depth in depths]
        + [
            pl.BlockSpec((width, depth), partial(lambda place, i: (0, place), place))
            for depth, place in zip(depths, places, strict=True)
        ],
        out_specs=pl.BlockSpec((tile, width), lambda i: (i, 0)),
        out_shape=jax.ShapeDtypeStruct((count, width), kind),
        cost_estimate=FREE,
        compiler_params=PARAMS,
    )(*lefts, *rights)


def turn(vectors, cosine, sine):
    lead = vectors[:, : HD // 2]
    lead = lead * cosine + pltpu.roll(lead, HD // 4, 1) * sine
    return jnp.concatenate([lead, vectors[:, HD // 2 :]], axis=1)


def attend_kernel(
    rows_ref, weight_ref, keys_ref, values_ref, allowed_ref, cosine_ref, sine_ref, queries_ref, context_ref, log_ref
):
    queries = dot(rows_ref[...], weight_ref[...], NN)
    queries = (turn(queries, cosine_ref[...], sine_ref[...]) * HD ** (-0.5)).astype(bf16)
    queries_ref[...] = queries
    scores = jnp.where(allowed_ref[...] > 0, dot(queries, keys_ref[...], NT), -1e30)
    peak = jnp.max(scores, axis=1, keepdims=True)
    powers = jnp.exp(scores - peak)
    total = jnp.sum(powers, axis=1, keepdims=True)
    probs_low = (powers / total).astype(bf16)
    context_ref[...] = dot(probs_low, values_ref[...], NN).astype(bf16)
    log_ref[...] = jnp.broadcast_to(peak + jnp.log(total), log_ref.shape)


def attend(rows, weights, keyvalue, allowed, cosine, sine, head_count):
    count, width = rows.shape
    length = keyvalue.shape[0]
    head = pl.BlockSpec((count, HD), lambda h: (0, h))
    table = pl.BlockSpec((count, HD // 2), lambda h: (0, 0))
    return pl.pallas_call(
        attend_kernel,
        grid=(head_count,),
        in_specs=[
            pl.BlockSpec((count, width), lambda h: (0, 0)),
            pl.BlockSpec((width, HD), lambda h: (0, h)),
            pl.BlockSpec((length, HD), lambda h: (0, 0)),
            pl.BlockSpec((length, HD), lambda h: (0, 1)),
            pl.BlockSpec((count, length), lambda h: (0, 0)),
            table,
            table,
        ],
        out_specs=[head, head, pl.BlockSpec((count, LANES), lambda h: (0, h))],
        out_shape=[jax.ShapeDtypeStruct((count, head_count * HD), bf16)] * 2
        + [jax.ShapeDtypeStruct((count, head_count * LANES), f32)],
        cost_estimate=FREE,
        compiler_params=PARAMS,
    )(rows, weights, keyvalue, keyvalue, allowed, cosine, sine)


def attend_back_kernel(
    rows_ref, weight_ref, queries_ref, log_ref, keys_ref, values_ref, allowed_ref, cosine_ref, sine_ref, query_ref, sums_ref
):
    context_grad = dot(rows_ref[...], weight_ref[...], NN).astype(bf16)
    queries, keys = queries_ref[...], keys_ref[...]
    scores = jnp.where(allowed_ref[...] > 0, dot(queries, keys, NT), -1e30)
    probs = jnp.exp(scores - log_ref[:, :1])
    probs_grad = dot(context_grad, values_ref[...], NT)
    prob_dot = jnp.sum(probs * probs_grad, axis=1, keepdims=True)
    score_grad = (probs * (probs_grad - prob_dot)).astype(bf16)
    query_grad = dot(score_grad, keys, NN) * HD ** (-0.5)
    query_ref[...] = turn(query_grad, cosine_ref[...], -sine_ref[...]).astype(bf16)

    @pl.when(pl.program_id(0) == 0)
    def _():
        sums_ref[...] = jnp.zeros_like(sums_ref)

    sums_ref[:, :HD] += dot(score_grad, queries, TN)
    sums_ref[:, HD:] += dot(probs.astype(bf16), context_grad, TN)


def attend_back(rows, weights, queries, logs, keyvalue, allowed, cosine, sine):
    count, width = rows.shape
    length = keyvalue.shape[0]
    head = pl.BlockSpec((count, HD), lambda h: (0, h))
    table = pl.BlockSpec((count, HD // 2), lambda h: (0, 0))
    return pl.pallas_call(
        attend_back_kernel,
        grid=(queries.shape[1] // HD,),
        in_specs=[
            pl.BlockSpec((count, width), lambda h: (0, 0)),
            pl.BlockSpec((width, HD), lambda h: (0, h)),
            head,
            pl.BlockSpec((count, LANES), lambda h: (0, h)),
            pl.BlockSpec((length, HD), lambda h: (0, 0)),
            pl.BlockSpec((length, HD), lambda h: (0, 1)),
            pl.BlockSpec((count, length), lambda h: (0, 0)),
            table,
            table,
        ],
        out_specs=[head, pl.BlockSpec((length, 2 * HD), lambda h: (0, 0))],
        out_shape=[
            jax.ShapeDtypeStruct(queries.shape, bf16),
            jax.ShapeDtypeStruct((length, 2 * HD), f32),
        ],
        cost_estimate=FREE,
        compiler_params=PARAMS,
    )(rows, weights, queries, logs, keyvalue, keyvalue, allowed, cosine, sine)


def weight_kernel(groups, half_ref, *refs):
    *pairs, out_ref = refs
    start = 0
    for lefts, rights in groups:
        size = pairs[rights[0]].shape[1]
        out_ref[:, start : start + size] = sum(
            dot(pairs[left][...], pairs[right][...], TN)
            for left, right in zip(lefts, rights, strict=True)
        ).astype(out_ref.dtype)
        start += size


def weight_out(half, *products):
    arrays, specs, groups, columns = [], [], [], 0
    count = products[0][1][0].shape[0]
    width = products[0][0][0].shape[1]
    tile = tile_of(width, 512)
    straight = pl.BlockSpec((count, tile), lambda i, half: (0, i))
    first = pl.BlockSpec((count, tile), lambda i, half: (half[0], i))
    second = pl.BlockSpec((count, tile), lambda i, half: (1 - half[0], i))
    known = {}
    for lefts, rights in products:
        halved = len(lefts) < len(rights)
        group = []
        for items, item_specs in (
            (lefts * 2 if halved else lefts, [first, second] if halved else [straight] * len(lefts)),
            (
                rights,
                [pl.BlockSpec((count, item.shape[1]), lambda i, half: (0, 0)) for item in rights],
            ),
        ):
            places = []
            for item, spec in zip(items, item_specs, strict=True):
                key = (id(item), id(spec) if halved else 0)
                if key not in known:
                    known[key] = len(arrays)
                    arrays.append(item)
                    specs.append(spec)
                places.append(known[key])
            group.append(places)
        groups.append(group)
        columns += rights[0].shape[1]
    return pl.pallas_call(
        partial(weight_kernel, groups),
        grid_spec=pltpu.PrefetchScalarGridSpec(
            num_scalar_prefetch=1,
            grid=(width // tile,),
            in_specs=specs,
            out_specs=pl.BlockSpec((tile, columns), lambda i, half: (i, 0)),
        ),
        out_shape=jax.ShapeDtypeStruct((width, columns), bf16),
        cost_estimate=FREE,
        compiler_params=PARAMS,
    )(half, *arrays)


def local(
    plan,
    block_input,
    segment_ids,
    output_grad,
    attention_gain,
    query_weight,
    keyvalue_weight,
    output_weight,
    output_bias,
    channel_gain,
    gate_weight,
    up_weight,
    down_weight,
    gate_bias,
    up_bias,
    down_bias,
):
    local_in = block_input[0].astype(f32)
    grad_local = output_grad[0]
    is_key = lax.axis_index("tensor") == 0
    ctx_index = lax.axis_index("y") * 2 + lax.axis_index("core")
    shard_rows = attention_gain.shape[0]
    token_count, width = local_in.shape
    ff_half = gate_bias.shape[0]
    blocks = plan.blocks
    block = -(-ff_half // (blocks * LANES)) * LANES
    ff_pad = blocks * block - ff_half

    segments = segment_ids[0]
    row_count = segments.shape[0]
    offsets = [0]
    for axis, mask in plan.ctx:
        segments = jnp.concatenate([segments, swap(segments, (axis, mask))])
        offsets = offsets + [item ^ (mask * 2 if axis == "y" else mask) for item in offsets]
    piece_index = jnp.arange(row_count, dtype=jnp.int32)
    key_index = jnp.concatenate([(ctx_index ^ item) * row_count + piece_index for item in offsets])
    own_segments = segments[:row_count]
    query_index = key_index[:row_count]
    earlier = jnp.sum((segments[None, :] < own_segments[:, None]).astype(jnp.int32), axis=1)
    cosine_table, sine_table = rotary_tables(query_index - earlier, HD)
    allowed = (
        (own_segments[:, None] == segments[None, :])
        & (key_index[None, :] <= query_index[:, None])
        & (query_index[:, None] - key_index[None, :] < WINDOW)
    ).astype(f32)
    cosine_both = jnp.concatenate([cosine_table, cosine_table], axis=1)
    sine_both = jnp.concatenate([-sine_table, sine_table], axis=1)

    def by_block(item):
        return lax.all_to_all(
            jnp.pad(item, ((0, 0), (0, ff_pad))),
            ("near",) + CTX,
            split_axis=1,
            concat_axis=0,
            tiled=True,
        )

    raw = block_input[0]
    raw_other = swap(raw, plan.tensor)
    down_rows, gate_rows, up_rows = (
        by_block(item) for item in (down_weight.T, gate_weight, up_weight)
    )

    vectors = jnp.stack([attention_gain, output_bias, channel_gain, down_bias], axis=1)
    vectors = jnp.pad(vectors, ((0, 0), (0, LANES - 4)))
    first = lax.all_gather(
        jnp.concatenate([query_weight, keyvalue_weight, vectors], axis=1),
        DP_CTX,
        axis=0,
        tiled=True,
    )
    full_output = lax.all_gather(output_weight.T, DP_CTX, axis=0, tiled=True)

    first, raw_other, *ff_rows = tie(first, raw_other, down_rows, gate_rows, up_rows)
    full_ff = []
    ff_in = Journey(repeat_in(ff_rows, plan, 2, full_ff))
    block_start = (lax.axis_index("near") * (blocks // 2) + ctx_index) * block
    pair_bias = jnp.stack(
        [
            lax.dynamic_slice_in_dim(jnp.pad(item, (0, ff_pad)), block_start, block)
            for item in (gate_bias, up_bias)
        ]
    ).astype(f32)

    query_columns, keyvalue_columns = query_weight.shape[1], keyvalue_weight.shape[1]
    full_keyvalue = first[:, query_columns : query_columns + keyvalue_columns]
    vectors = first[:, query_columns + keyvalue_columns :].astype(f32)
    gain_one, full_obias, gain_two, full_dbias = (vectors[:, i] for i in range(4))
    norm_one_pull = jax.vjp(norm_scale, local_in, gain_one)[1]
    raw_rows = jnp.concatenate(in_order(plan.tensor, raw, raw_other), axis=0)
    normed = norm_scale(raw_rows.astype(f32), gain_one).astype(bf16)
    head_count = query_columns // HD
    half_proj = jnp.dot(normed, full_keyvalue, preferred_element_type=f32)
    half_low = jnp.where(
        is_key, rotate(half_proj[:, None, :], cosine_table, sine_table, 1.0)[:, 0], half_proj
    ).astype(bf16)
    keyvalue = jnp.concatenate(in_order(plan.tensor, half_low, swap(half_low, plan.tensor)), axis=1)
    for bit in plan.ctx:
        keyvalue = jnp.concatenate([keyvalue, swap(keyvalue, bit)], axis=0)
        if bit == plan.y[-1]:
            keyvalue = ff_in.step(keyvalue)
    all_grads = lax.all_gather(
        grad_local, ("core", "near", "y", "tensor"), axis=0, tiled=True
    )
    keyvalue = ff_in.step(keyvalue)
    queries, context, logs = attend(
        normed, first, keyvalue, allowed, cosine_both, sine_both, head_count
    )
    attended = rows_out([context], [full_output], f32)
    attended, grad_low = ff_in.step((attended, grad_local))
    mixed = local_in + sum_rows(attended, plan) + full_obias
    mixed = ff_in.step(mixed)

    normed_two_local, norm_two_pull = jax.vjp(norm_scale, mixed, gain_two)
    journey = Journey(gather_tokens(normed_two_local.astype(bf16), plan))
    mixed = ff_in.step(journey.step(mixed))
    mixed = ff_in.finish(journey.step(mixed))
    mixed, full_ff = tie(mixed, full_ff)
    mixed = journey.finish(mixed)
    normed_two = journey.result
    full_down, full_gate, full_up = full_ff
    core = lax.axis_index("core")
    own_half, other_half = (jnp.full((1,), item, jnp.int32) for item in (core, 1 - core))
    weights = (full_gate, full_up, full_down, pair_bias)
    own_part = hidden_units(own_half, normed_two[0], all_grads, *weights)
    normed_two[1], own_part = tie(normed_two[1], own_part)
    parts = [own_part, hidden_units(other_half, normed_two[1], all_grads, *weights)]
    hidden, gate_grad, up_grad, bias_sums = (list(item) for item in zip(*parts, strict=True))
    pair_weights = [full_gate, full_up]
    two_other = rows_out([gate_grad[1], up_grad[1]], pair_weights)
    ff_small = Journey(spread_small(sum(bias_sums), plan))
    two_other, gate_grad, up_grad = tie(two_other, gate_grad, up_grad)
    two_own = rows_out([gate_grad[0], up_grad[0]], pair_weights)
    two_own = ff_small.step(two_own)
    two_sum = Journey(reduce_tokens(two_own, two_other, plan, token_count))
    gate_grad, up_grad, hidden = two_sum.step((gate_grad, up_grad, hidden))
    ff_wgrad = weight_out(
        own_half, ([all_grads], hidden), (normed_two, gate_grad), (normed_two, up_grad)
    )
    ff_wgrad, hidden = ff_small.step(two_sum.step((ff_wgrad, hidden)))
    ff_sum = lax.psum_scatter(ff_wgrad, "far", scatter_dimension=0, tiled=True)
    hidden = ff_small.step(two_sum.step(hidden))
    hidden = two_sum.finish(hidden)
    two_grad = two_sum.result

    grad_full = grad_local.astype(f32)
    dbias_part = jnp.sum(grad_full, axis=0)
    mixed_part, gain_two_part = norm_two_pull(two_grad)
    mixed_grad = grad_full + mixed_part
    obias_part = jnp.sum(mixed_grad, axis=0)
    mixed_low = mixed_grad.astype(bf16)
    mixed_other = swap(mixed_low, plan.tensor)
    hidden, mixed_low = tie(hidden, mixed_low)
    out_other = rows_out([hidden[1]], [full_down])
    out_other, hidden = tie(out_other, hidden)
    out_own = rows_out([hidden[0]], [full_down])
    out_sum = Journey(reduce_tokens(out_own, out_other, plan, token_count))
    mixed_other, out_own = tie(mixed_other, out_own)
    attn_rows = jnp.concatenate(in_order(plan.tensor, mixed_low, mixed_other), axis=0)
    order_one = plan.ctx[::-1] + plan.near + plan.far[::-1]
    order_two = [plan.core] + plan.near + plan.y[::-1] + plan.far[::-1]
    attn_rows = ff_small.finish(out_sum.step(attn_rows))
    query_proj_grad, stacked = attend_back(
        attn_rows, full_output, queries, logs, keyvalue, allowed, cosine_both, sine_both
    )
    stacked, query_proj_grad, attn_rows = tie(stacked, query_proj_grad, attn_rows)
    query_wgrad = weight_out(own_half, ([normed], [query_proj_grad]))
    for bit in reversed(plan.ctx):
        half = stacked.shape[0] // 2
        other = swap(stacked[half:].astype(bf16), bit)
        if bit == plan.core:
            other, query_wgrad, attn_rows = tie(other, query_wgrad, attn_rows)
            query_sum = Journey(reduce_rows([query_wgrad], plan, [order_one]))
            output_wgrad = weight_out(own_half, ([attn_rows], [context]))
        elif bit == plan.y[-1]:
            other, output_wgrad = query_sum.step(out_sum.step((other, output_wgrad)))
        stacked = stacked[:half] + other.astype(f32)
    mine, theirs = halves(stacked, plan.tensor, 1)
    half_grad = mine + swap(theirs.astype(bf16), plan.tensor).astype(f32)
    half_grad = jnp.where(
        is_key, rotate(half_grad[:, None, :], cosine_table, sine_table, -1.0)[:, 0], half_grad
    ).astype(bf16)
    one_part = rows_out([query_proj_grad, half_grad], [first, first], f32, [0, query_columns])
    mine, theirs = halves(one_part, plan.tensor, 0)
    theirs, half_grad, output_wgrad = tie(theirs.astype(bf16), half_grad, output_wgrad)
    other = swap(theirs, plan.tensor)
    keyvalue_wgrad = weight_out(own_half, ([normed], [half_grad]))
    other, keyvalue_wgrad, output_wgrad = out_sum.step((other, keyvalue_wgrad, output_wgrad))
    input_part, gain_one_part = norm_one_pull(mine + other.astype(f32))
    input_grad = mixed_grad + input_part
    input_grad, output_wgrad, keyvalue_wgrad = out_sum.finish(
        (input_grad, output_wgrad, keyvalue_wgrad)
    )
    block_output = (mixed + out_sum.result + full_dbias).astype(bf16)

    small = jnp.stack([gain_one_part, gain_two_part, obias_part, dbias_part], axis=0)
    small = small + swap(small, plan.tensor)
    small = jnp.pad(small.T.astype(bf16), ((0, 0), (0, LANES - 4)))
    keyvalue_wgrad = jnp.concatenate([keyvalue_wgrad, small], axis=1)
    keyvalue_sum = Journey(reduce_rows([keyvalue_wgrad], plan, [order_one]))
    input_grad = query_sum.step(input_grad)
    output_wgrad, input_grad = tie(output_wgrad, input_grad)
    output_sum = Journey(reduce_rows([output_wgrad], plan, [order_one]))
    input_grad = output_sum.step(input_grad)
    input_grad = keyvalue_sum.step(input_grad)
    ff_sum, input_grad = tie(ff_sum, input_grad)
    y_first = [plan.core] + plan.y[::-1] + plan.near[::-1]
    near_first = [plan.core] + plan.near[::-1] + plan.y[::-1]
    backs = [
        Journey(spread_back(ff_sum[:, i * block : (i + 1) * block], plan, bits))
        for i, bits in enumerate((y_first, y_first, near_first))
    ]
    input_grad = backs[0].step(input_grad)
    input_grad = backs[1].step(input_grad)
    input_grad = backs[2].step(input_grad)
    input_grad = query_sum.step(input_grad)
    input_grad = keyvalue_sum.step(input_grad)
    input_grad = finish_all([output_sum, *backs, query_sum, keyvalue_sum], input_grad)
    proj_out = output_sum.result[0]
    query_out = query_sum.result[0]
    keyvalue_out = keyvalue_sum.result[0][:, :keyvalue_columns]
    small = keyvalue_sum.result[0][:, keyvalue_columns : keyvalue_columns + 4].T
    ff_small = ff_small.result
    down_out, gate_out, up_out = (item.result[:, :ff_half].astype(f32) for item in backs)
    return (
        block_output[None],
        input_grad[None],
        small[0],
        query_out,
        keyvalue_out,
        proj_out.T,
        small[2],
        small[1],
        gate_out,
        up_out,
        down_out.T,
        ff_small[0, :ff_half],
        ff_small[1, :ff_half],
        small[3],
    )


def solution(mesh):
    near = 2
    shape = (mesh.shape["dp"] // near, near, mesh.shape["ctx"] // 2, 2, mesh.shape["tensor"])
    names = DP + CTX + ("tensor",)
    mesh = Mesh(mesh.devices.reshape(shape), names)
    plan = Plan(dict(zip(names, shape, strict=True)))
    rows = P(DP, CTX + ("tensor",), None)
    vector = P(DP_CTX)
    wide = P(DP_CTX, "tensor")
    tall = P("tensor", DP_CTX)
    units = P("tensor")
    return jax.shard_map(
        partial(local, plan),
        mesh=mesh,
        in_specs=(
            rows,
            P(DP, CTX),
            rows,
            vector,
            wide,
            wide,
            tall,
            vector,
            vector,
            wide,
            wide,
            tall,
            units,
            units,
            vector,
        ),
        out_specs=(
            rows,
            rows,
            vector,
            wide,
            wide,
            tall,
            vector,
            vector,
            wide,
            wide,
            tall,
            units,
            units,
            vector,
        ),
        check_vma=False,
    )
```

```python
from functools import partial
import math

import jax
import jax.numpy as jnp
from jax import lax
from jax.experimental import pallas as pl
from jax.experimental.pallas import tpu as pltpu
from jax.sharding import Mesh
from jax.sharding import PartitionSpec as P

HD = 256
WINDOW = 2048
LANES = 128
GELU_SCALE = math.sqrt(2.0 / math.pi)
GELU_CUBE = 0.044715
DP = ("far", "near")
CTX = ("y", "core")
DP_CTX = DP + CTX
f32 = jnp.float32
bf16 = jnp.bfloat16


def norm_scale(vectors, scale_gain):
    return (
        vectors
        * lax.rsqrt(jnp.mean(vectors * vectors, axis=-1, keepdims=True) + 1e-06)
        * scale_gain
    )


def rotary_tables(positions, head_size):
    quarter = head_size // 4
    frequency = jnp.exp(jnp.arange(quarter, dtype=jnp.float32) * (-math.log(10000.0) / quarter))
    angles = positions.astype(jnp.float32)[:, None] * frequency[None, :]
    return (jnp.cos(angles), jnp.sin(angles))


def rotate(vectors, cosine_table, sine_table, direction):
    quarter = cosine_table.shape[-1]
    lead_part = vectors[..., :quarter]
    trail_part = vectors[..., quarter : 2 * quarter]
    cosine_wide = cosine_table[:, None, :]
    sine_wide = direction * sine_table[:, None, :]
    return jnp.concatenate(
        [
            lead_part * cosine_wide - trail_part * sine_wide,
            trail_part * cosine_wide + lead_part * sine_wide,
            vectors[..., 2 * quarter :],
        ],
        axis=-1,
    )


def bits_of(axis, size):
    masks = []
    while size > 1:
        size //= 2
        masks.append((axis, size))
    return masks


def swap(values, bit):
    axis, mask = bit
    return lax.ppermute(values, axis, [(i, i ^ mask) for i in range(lax.axis_size(axis))])


def digit(bit):
    axis, mask = bit
    return (lax.axis_index(axis) // mask) % 2


def in_order(bit, mine, other):
    one = digit(bit) == 1
    return jnp.where(one, other, mine), jnp.where(one, mine, other)


def halves(values, bit, axis):
    size = values.shape[axis] // 2
    own = digit(bit)
    return (
        lax.dynamic_slice_in_dim(values, own * size, size, axis),
        lax.dynamic_slice_in_dim(values, (1 - own) * size, size, axis),
    )


def tie(*groups):
    return lax.optimization_barrier(groups)


def finish_all(items, hold):
    while any(item.result is None for item in items):
        for item in items:
            if item.result is None:
                hold = item.step(hold)
    return hold


def tie_to(values, hold):
    return (values, None) if hold is None else tie(values, hold)


class Plan:
    def __init__(self, sizes):
        self.far = bits_of("far", sizes["far"])
        self.near = bits_of("near", sizes["near"])
        self.y = bits_of("y", sizes["y"])
        self.core = ("core", 1)
        self.tensor = ("tensor", 1)
        self.ctx = self.y + [self.core]
        self.rows = self.far + self.near + self.ctx
        self.links = [self.tensor] + self.y + self.near
        self.chip = self.near + self.y + [self.tensor]
        self.blocks = sizes["near"] * sizes["y"] * 2


class Journey:
    def __init__(self, steps):
        self.steps = steps
        self.result = None
        next(steps)

    def step(self, hold):
        try:
            return self.steps.send(hold)
        except StopIteration as end:
            self.result, hold = end.value
            return hold

    def finish(self, hold):
        while self.result is None:
            hold = self.step(hold)
        return hold


def repeat_in(arrays, plan, cuts, whole):
    hold = None
    for rows in arrays:
        size = rows.shape[0] // cuts
        pieces = []
        for start in range(0, rows.shape[0], size):
            piece = rows[start : start + size]
            if hold is not None:
                piece, hold = tie(piece, hold)
            for bit in reversed(plan.far):
                other = swap(piece, bit)
                hold = yield hold
                other, hold = tie_to(other, hold)
                piece = jnp.concatenate(in_order(bit, piece, other), axis=0)
            pieces.append(piece.reshape(-1, size, rows.shape[1]))
        whole.append(jnp.concatenate(pieces, axis=1).reshape(-1, rows.shape[1]))
    return whole, hold


def spread_back(grad, plan, bits):
    hold = None
    columns = grad.shape[-1]
    present = plan.near + plan.ctx
    grad = grad.reshape((2,) * len(present) + (-1, columns))
    for bit in bits:
        place = present.index(bit)
        present = present[:place] + present[place + 1 :]
        mine, theirs = halves(grad, bit, place)
        other = swap(jnp.squeeze(theirs, place), bit)
        hold = yield hold
        other, hold = tie_to(other, hold)
        grad = jnp.concatenate(in_order(bit, jnp.squeeze(mine, place), other), axis=-1)
    order = bits[::-1]
    if order != plan.near + plan.ctx:
        grad = grad.reshape((grad.shape[0],) + (2,) * len(bits) + (columns,))
        axes = [1 + order.index(bit) for bit in plan.near + plan.ctx]
        grad = grad.transpose([0] + axes + [len(bits) + 1]).reshape(grad.shape[0], -1)
    return grad, hold


def reduce_rows(grads, plan, orders, kind=bf16):
    hold = None
    states = [
        (grad.reshape((2,) * len(plan.rows) + (-1, grad.shape[-1])), list(plan.rows))
        for grad in grads
    ]
    for step in range(len(plan.rows)):
        kept, others = [], []
        for (grad, present), order in zip(states, orders, strict=True):
            place = present.index(order[step])
            mine, theirs = halves(grad, order[step], place)
            kept.append((jnp.squeeze(mine, place), present[:place] + present[place + 1 :]))
            others.append(jnp.squeeze(swap(theirs.astype(kind), order[step]), place))
        hold = yield hold
        others, hold = tie_to(others, hold)
        states = []
        for (mine, present), other in zip(kept, others, strict=True):
            grad = mine.astype(f32) + other.astype(f32)
            states.append((grad.astype(kind) if present else grad, present))
    return [grad for grad, _ in states], hold


def spread_small(part, plan):
    hold = None
    for bit in plan.far:
        other = swap(part, bit)
        hold = yield hold
        other, hold = tie_to(other, hold)
        part = part + other
    for bit in reversed(plan.near + plan.ctx):
        other = swap(part, bit)
        hold = yield hold
        other, hold = tie_to(other, hold)
        part = jnp.concatenate(in_order(bit, part, other), axis=1)
    return part, hold


def token_parts(count, plan):
    links = len(plan.links)
    step = 16
    units = count // step
    sizes = [(units + i) // links * step for i in range(links)]
    parts = []
    start = 0
    for i, size in enumerate(sizes):
        if size:
            parts.append((start, size, plan.links[i:] + plan.links[:i]))
            start += size
    return parts


def gather_tokens(local_rows, plan):
    hold = None
    parts = token_parts(local_rows.shape[0], plan)
    pieces = [(local_rows[start : start + size], []) for start, size, _ in parts]
    for step in range(len(plan.links)):
        bits = [order[step] for _, _, order in parts]
        others = [swap(piece, bit) for (piece, _), bit in zip(pieces, bits, strict=True)]
        hold = yield hold
        others, hold = tie_to(others, hold)
        grown = []
        for (piece, present), bit, other in zip(pieces, bits, others, strict=True):
            place = sum(1 for done in present if plan.chip.index(done) < plan.chip.index(bit))
            grown.append((jnp.stack(in_order(bit, piece, other), axis=place), present + [bit]))
        pieces = grown
    chip = jnp.concatenate([piece for piece, _ in pieces], axis=-2).reshape(
        -1, local_rows.shape[1]
    )
    return [chip, swap(chip, plan.core)], hold


def reduce_tokens(own, other, plan, count):
    got = swap(other, plan.core)
    hold = yield None
    got, hold = tie_to(got, hold)
    chip = (own.astype(f32) + got.astype(f32)).astype(bf16)
    chip = chip.reshape((2,) * len(plan.chip) + (count, -1))
    parts = token_parts(count, plan)
    pieces = [
        (lax.slice_in_dim(chip, start, start + size, axis=chip.ndim - 2), list(plan.chip))
        for start, size, _ in parts
    ]
    for step in reversed(range(len(plan.links))):
        kept, others = [], []
        for (piece, present), (_, _, order) in zip(pieces, parts, strict=True):
            place = present.index(order[step])
            mine, theirs = halves(piece, order[step], place)
            kept.append((jnp.squeeze(mine, place), present[:place] + present[place + 1 :]))
            others.append(swap(jnp.squeeze(theirs, place), order[step]))
        hold = yield hold
        others, hold = tie_to(others, hold)
        pieces = []
        for (mine, present), got in zip(kept, others, strict=True):
            piece = mine.astype(f32) + got.astype(f32)
            pieces.append((piece.astype(bf16) if present else piece, present))
    return jnp.concatenate([piece for piece, _ in pieces], axis=0), hold


def gather_rows(values_low, plan):
    return jnp.concatenate(in_order(plan.tensor, values_low, swap(values_low, plan.tensor)), axis=0)


def sum_rows(partial_rows, plan):
    mine, theirs = halves(partial_rows, plan.tensor, 0)
    return mine.astype(f32) + swap(theirs.astype(bf16), plan.tensor).astype(f32)


FREE = pl.CostEstimate(flops=0, bytes_accessed=0, transcendentals=0)
PARAMS = pltpu.CompilerParams(vmem_limit_bytes=48 * 2**20)
NN = (((1,), (0,)), ((), ()))
NT = (((1,), (1,)), ((), ()))
TN = (((0,), (0,)), ((), ()))


def dot(left, right, dims):
    return lax.dot_general(left, right, dims, preferred_element_type=f32)


def tile_of(size, most):
    return max(tile for tile in range(LANES, most + 1, LANES) if size % tile == 0)


def hidden_kernel(
    half_ref, rows_ref, grad_ref, gate_ref, up_ref, down_ref, bias_ref, hidden_ref, gate_grad_ref, up_grad_ref, sums_ref
):
    gate = dot(rows_ref[...], gate_ref[...], NN) + bias_ref[0:1]
    up = dot(rows_ref[...], up_ref[...], NN) + bias_ref[1:2]
    hidden_grad = dot(grad_ref[...], down_ref[...], NN)
    square = gate * gate
    bend = jnp.tanh(GELU_SCALE * gate * (1.0 + GELU_CUBE * square))
    half = 0.5 * (1.0 + bend)
    activated = gate * half
    slope = half + 0.5 * gate * (1.0 - bend * bend) * (
        GELU_SCALE * (1.0 + 3.0 * GELU_CUBE * square)
    )
    hidden_ref[...] = (activated * up).astype(bf16)
    gate_grad = hidden_grad * up * slope
    up_grad = hidden_grad * activated
    gate_grad_ref[...] = gate_grad.astype(bf16)
    up_grad_ref[...] = up_grad.astype(bf16)

    @pl.when(pl.program_id(0) == 0)
    def _():
        sums_ref[...] = jnp.zeros_like(sums_ref)

    sums_ref[0:1] += jnp.sum(gate_grad, axis=0, keepdims=True)
    sums_ref[1:2] += jnp.sum(up_grad, axis=0, keepdims=True)


def hidden_units(half, rows, grads, gate, up, down, bias):
    count, width = rows.shape
    block = gate.shape[1]
    tile = tile_of(count, 256)
    weight_spec = pl.BlockSpec((width, block), lambda i, half: (0, 0))
    unit_spec = pl.BlockSpec((tile, block), lambda i, half: (i, 0))
    pair_spec = pl.BlockSpec((2, block), lambda i, half: (0, 0))
    return pl.pallas_call(
        hidden_kernel,
        grid_spec=pltpu.PrefetchScalarGridSpec(
            num_scalar_prefetch=1,
            grid=(count // tile,),
            in_specs=[
                pl.BlockSpec((tile, width), lambda i, half: (i, 0)),
                pl.BlockSpec((tile, width), lambda i, half: (half[0] * (count // tile) + i, 0)),
                weight_spec,
                weight_spec,
                weight_spec,
                pair_spec,
            ],
            out_specs=[unit_spec, unit_spec, unit_spec, pair_spec],
        ),
        out_shape=[jax.ShapeDtypeStruct((count, block), bf16)] * 3
        + [jax.ShapeDtypeStruct((2, block), f32)],
        cost_estimate=FREE,
        compiler_params=PARAMS,
    )(half, rows, grads, gate, up, down, bias)


def rows_kernel(*refs):
    *pairs, out_ref = refs
    half = len(pairs) // 2
    out_ref[...] = sum(
        dot(left[...], right[...], NT)
        for left, right in zip(pairs[:half], pairs[half:], strict=True)
    ).astype(out_ref.dtype)


def rows_out(lefts, rights, kind=bf16, starts=None):
    count = lefts[0].shape[0]
    width = rights[0].shape[0]
    tile = tile_of(count, 256)
    depths = [item.shape[1] for item in lefts]
    places = [start // depth for start, depth in zip(starts or [0] * len(lefts), depths, strict=True)]
    return pl.pallas_call(
        rows_kernel,
        grid=(count // tile,),
        in_specs=[pl.BlockSpec((tile, depth), lambda i: (i, 0)) for depth in depths]
        + [
            pl.BlockSpec((width, depth), partial(lambda place, i: (0, place), place))
            for depth, place in zip(depths, places, strict=True)
        ],
        out_specs=pl.BlockSpec((tile, width), lambda i: (i, 0)),
        out_shape=jax.ShapeDtypeStruct((count, width), kind),
        cost_estimate=FREE,
        compiler_params=PARAMS,
    )(*lefts, *rights)


def turn(vectors, cosine, sine):
    lead = vectors[:, : HD // 2]
    lead = lead * cosine + pltpu.roll(lead, HD // 4, 1) * sine
    return jnp.concatenate([lead, vectors[:, HD // 2 :]], axis=1)


def attend_kernel(
    rows_ref, weight_ref, keys_ref, values_ref, allowed_ref, cosine_ref, sine_ref, queries_ref, context_ref, log_ref
):
    queries = dot(rows_ref[...], weight_ref[...], NN)
    queries = (turn(queries, cosine_ref[...], sine_ref[...]) * HD ** (-0.5)).astype(bf16)
    queries_ref[...] = queries
    scores = jnp.where(allowed_ref[...] > 0, dot(queries, keys_ref[...], NT), -1e30)
    peak = jnp.max(scores, axis=1, keepdims=True)
    powers = jnp.exp(scores - peak)
    total = jnp.sum(powers, axis=1, keepdims=True)
    probs_low = (powers / total).astype(bf16)
    context_ref[...] = dot(probs_low, values_ref[...], NN).astype(bf16)
    log_ref[...] = jnp.broadcast_to(peak + jnp.log(total), log_ref.shape)


def attend(rows, weights, keyvalue, allowed, cosine, sine, head_count):
    count, width = rows.shape
    length = keyvalue.shape[0]
    head = pl.BlockSpec((count, HD), lambda h: (0, h))
    table = pl.BlockSpec((count, HD // 2), lambda h: (0, 0))
    return pl.pallas_call(
        attend_kernel,
        grid=(head_count,),
        in_specs=[
            pl.BlockSpec((count, width), lambda h: (0, 0)),
            pl.BlockSpec((width, HD), lambda h: (0, h)),
            pl.BlockSpec((length, HD), lambda h: (0, 0)),
            pl.BlockSpec((length, HD), lambda h: (0, 1)),
            pl.BlockSpec((count, length), lambda h: (0, 0)),
            table,
            table,
        ],
        out_specs=[head, head, pl.BlockSpec((count, LANES), lambda h: (0, h))],
        out_shape=[jax.ShapeDtypeStruct((count, head_count * HD), bf16)] * 2
        + [jax.ShapeDtypeStruct((count, head_count * LANES), f32)],
        cost_estimate=FREE,
        compiler_params=PARAMS,
    )(rows, weights, keyvalue, keyvalue, allowed, cosine, sine)


def attend_back_kernel(
    rows_ref, weight_ref, queries_ref, log_ref, keys_ref, values_ref, allowed_ref, cosine_ref, sine_ref, query_ref, sums_ref
):
    context_grad = dot(rows_ref[...], weight_ref[...], NN).astype(bf16)
    queries, keys = queries_ref[...], keys_ref[...]
    scores = jnp.where(allowed_ref[...] > 0, dot(queries, keys, NT), -1e30)
    probs = jnp.exp(scores - log_ref[:, :1])
    probs_grad = dot(context_grad, values_ref[...], NT)
    prob_dot = jnp.sum(probs * probs_grad, axis=1, keepdims=True)
    score_grad = (probs * (probs_grad - prob_dot)).astype(bf16)
    query_grad = dot(score_grad, keys, NN) * HD ** (-0.5)
    query_ref[...] = turn(query_grad, cosine_ref[...], -sine_ref[...]).astype(bf16)

    @pl.when(pl.program_id(0) == 0)
    def _():
        sums_ref[...] = jnp.zeros_like(sums_ref)

    sums_ref[:, :HD] += dot(score_grad, queries, TN)
    sums_ref[:, HD:] += dot(probs.astype(bf16), context_grad, TN)


def attend_back(rows, weights, queries, logs, keyvalue, allowed, cosine, sine):
    count, width = rows.shape
    length = keyvalue.shape[0]
    head = pl.BlockSpec((count, HD), lambda h: (0, h))
    table = pl.BlockSpec((count, HD // 2), lambda h: (0, 0))
    return pl.pallas_call(
        attend_back_kernel,
        grid=(queries.shape[1] // HD,),
        in_specs=[
            pl.BlockSpec((count, width), lambda h: (0, 0)),
            pl.BlockSpec((width, HD), lambda h: (0, h)),
            head,
            pl.BlockSpec((count, LANES), lambda h: (0, h)),
            pl.BlockSpec((length, HD), lambda h: (0, 0)),
            pl.BlockSpec((length, HD), lambda h: (0, 1)),
            pl.BlockSpec((count, length), lambda h: (0, 0)),
            table,
            table,
        ],
        out_specs=[head, pl.BlockSpec((length, 2 * HD), lambda h: (0, 0))],
        out_shape=[
            jax.ShapeDtypeStruct(queries.shape, bf16),
            jax.ShapeDtypeStruct((length, 2 * HD), f32),
        ],
        cost_estimate=FREE,
        compiler_params=PARAMS,
    )(rows, weights, queries, logs, keyvalue, keyvalue, allowed, cosine, sine)


def weight_kernel(groups, half_ref, *refs):
    *pairs, out_ref = refs
    start = 0
    for lefts, rights in groups:
        size = pairs[rights[0]].shape[1]
        out_ref[:, start : start + size] = sum(
            dot(pairs[left][...], pairs[right][...], TN)
            for left, right in zip(lefts, rights, strict=True)
        ).astype(out_ref.dtype)
        start += size


def weight_out(half, *products):
    arrays, specs, groups, columns = [], [], [], 0
    count = products[0][1][0].shape[0]
    width = products[0][0][0].shape[1]
    tile = tile_of(width, 512)
    straight = pl.BlockSpec((count, tile), lambda i, half: (0, i))
    first = pl.BlockSpec((count, tile), lambda i, half: (half[0], i))
    second = pl.BlockSpec((count, tile), lambda i, half: (1 - half[0], i))
    known = {}
    for lefts, rights in products:
        halved = len(lefts) < len(rights)
        group = []
        for items, item_specs in (
            (lefts * 2 if halved else lefts, [first, second] if halved else [straight] * len(lefts)),
            (
                rights,
                [pl.BlockSpec((count, item.shape[1]), lambda i, half: (0, 0)) for item in rights],
            ),
        ):
            places = []
            for item, spec in zip(items, item_specs, strict=True):
                key = (id(item), id(spec) if halved else 0)
                if key not in known:
                    known[key] = len(arrays)
                    arrays.append(item)
                    specs.append(spec)
                places.append(known[key])
            group.append(places)
        groups.append(group)
        columns += rights[0].shape[1]
    return pl.pallas_call(
        partial(weight_kernel, groups),
        grid_spec=pltpu.PrefetchScalarGridSpec(
            num_scalar_prefetch=1,
            grid=(width // tile,),
            in_specs=specs,
            out_specs=pl.BlockSpec((tile, columns), lambda i, half: (i, 0)),
        ),
        out_shape=jax.ShapeDtypeStruct((width, columns), bf16),
        cost_estimate=FREE,
        compiler_params=PARAMS,
    )(half, *arrays)


def local(
    plan,
    block_input,
    segment_ids,
    output_grad,
    attention_gain,
    query_weight,
    keyvalue_weight,
    output_weight,
    output_bias,
    channel_gain,
    gate_weight,
    up_weight,
    down_weight,
    gate_bias,
    up_bias,
    down_bias,
):
    local_in = block_input[0].astype(f32)
    grad_local = output_grad[0]
    is_key = lax.axis_index("tensor") == 0
    ctx_index = lax.axis_index("y") * 2 + lax.axis_index("core")
    shard_rows = attention_gain.shape[0]
    token_count, width = local_in.shape
    ff_half = gate_bias.shape[0]
    blocks = plan.blocks
    block = -(-ff_half // (blocks * LANES)) * LANES
    ff_pad = blocks * block - ff_half

    segments = segment_ids[0]
    row_count = segments.shape[0]
    offsets = [0]
    for axis, mask in plan.ctx:
        segments = jnp.concatenate([segments, swap(segments, (axis, mask))])
        offsets = offsets + [item ^ (mask * 2 if axis == "y" else mask) for item in offsets]
    piece_index = jnp.arange(row_count, dtype=jnp.int32)
    key_index = jnp.concatenate([(ctx_index ^ item) * row_count + piece_index for item in offsets])
    own_segments = segments[:row_count]
    query_index = key_index[:row_count]
    earlier = jnp.sum((segments[None, :] < own_segments[:, None]).astype(jnp.int32), axis=1)
    cosine_table, sine_table = rotary_tables(query_index - earlier, HD)
    allowed = (
        (own_segments[:, None] == segments[None, :])
        & (key_index[None, :] <= query_index[:, None])
        & (query_index[:, None] - key_index[None, :] < WINDOW)
    ).astype(f32)
    cosine_both = jnp.concatenate([cosine_table, cosine_table], axis=1)
    sine_both = jnp.concatenate([-sine_table, sine_table], axis=1)

    def by_block(item):
        return lax.all_to_all(
            jnp.pad(item, ((0, 0), (0, ff_pad))),
            ("near",) + CTX,
            split_axis=1,
            concat_axis=0,
            tiled=True,
        )

    raw = block_input[0]
    raw_other = swap(raw, plan.tensor)
    down_rows, gate_rows, up_rows = (
        by_block(item) for item in (down_weight.T, gate_weight, up_weight)
    )

    vectors = jnp.stack([attention_gain, output_bias, channel_gain, down_bias], axis=1)
    vectors = jnp.pad(vectors, ((0, 0), (0, LANES - 4)))
    first = lax.all_gather(
        jnp.concatenate([query_weight, keyvalue_weight, vectors], axis=1),
        DP_CTX,
        axis=0,
        tiled=True,
    )
    full_output = lax.all_gather(output_weight.T, DP_CTX, axis=0, tiled=True)

    first, raw_other, *ff_rows = tie(first, raw_other, down_rows, gate_rows, up_rows)
    full_ff = []
    ff_in = Journey(repeat_in(ff_rows, plan, 2, full_ff))
    block_start = (lax.axis_index("near") * (blocks // 2) + ctx_index) * block
    pair_bias = jnp.stack(
        [
            lax.dynamic_slice_in_dim(jnp.pad(item, (0, ff_pad)), block_start, block)
            for item in (gate_bias, up_bias)
        ]
    ).astype(f32)

    query_columns, keyvalue_columns = query_weight.shape[1], keyvalue_weight.shape[1]
    full_keyvalue = first[:, query_columns : query_columns + keyvalue_columns]
    vectors = first[:, query_columns + keyvalue_columns :].astype(f32)
    gain_one, full_obias, gain_two, full_dbias = (vectors[:, i] for i in range(4))
    norm_one_pull = jax.vjp(norm_scale, local_in, gain_one)[1]
    raw_rows = jnp.concatenate(in_order(plan.tensor, raw, raw_other), axis=0)
    normed = norm_scale(raw_rows.astype(f32), gain_one).astype(bf16)
    head_count = query_columns // HD
    half_proj = jnp.dot(normed, full_keyvalue, preferred_element_type=f32)
    half_low = jnp.where(
        is_key, rotate(half_proj[:, None, :], cosine_table, sine_table, 1.0)[:, 0], half_proj
    ).astype(bf16)
    keyvalue = jnp.concatenate(in_order(plan.tensor, half_low, swap(half_low, plan.tensor)), axis=1)
    for bit in plan.ctx:
        keyvalue = jnp.concatenate([keyvalue, swap(keyvalue, bit)], axis=0)
        if bit == plan.y[-1]:
            keyvalue = ff_in.step(keyvalue)
    all_grads = lax.all_gather(
        grad_local, ("core", "near", "y", "tensor"), axis=0, tiled=True
    )
    keyvalue = ff_in.step(keyvalue)
    queries, context, logs = attend(
        normed, first, keyvalue, allowed, cosine_both, sine_both, head_count
    )
    attended = rows_out([context], [full_output], f32)
    attended, grad_low = ff_in.step((attended, grad_local))
    mixed = local_in + sum_rows(attended, plan) + full_obias
    mixed = ff_in.step(mixed)

    normed_two_local, norm_two_pull = jax.vjp(norm_scale, mixed, gain_two)
    journey = Journey(gather_tokens(normed_two_local.astype(bf16), plan))
    mixed = ff_in.step(journey.step(mixed))
    mixed = ff_in.finish(journey.step(mixed))
    mixed, full_ff = tie(mixed, full_ff)
    mixed = journey.finish(mixed)
    normed_two = journey.result
    full_down, full_gate, full_up = full_ff
    core = lax.axis_index("core")
    own_half, other_half = (jnp.full((1,), item, jnp.int32) for item in (core, 1 - core))
    weights = (full_gate, full_up, full_down, pair_bias)
    own_part = hidden_units(own_half, normed_two[0], all_grads, *weights)
    normed_two[1], own_part = tie(normed_two[1], own_part)
    parts = [own_part, hidden_units(other_half, normed_two[1], all_grads, *weights)]
    hidden, gate_grad, up_grad, bias_sums = (list(item) for item in zip(*parts, strict=True))
    pair_weights = [full_gate, full_up]
    two_other = rows_out([gate_grad[1], up_grad[1]], pair_weights)
    ff_small = Journey(spread_small(sum(bias_sums), plan))
    two_other, gate_grad, up_grad = tie(two_other, gate_grad, up_grad)
    two_own = rows_out([gate_grad[0], up_grad[0]], pair_weights)
    two_own = ff_small.step(two_own)
    two_sum = Journey(reduce_tokens(two_own, two_other, plan, token_count))
    gate_grad, up_grad, hidden = two_sum.step((gate_grad, up_grad, hidden))
    ff_wgrad = weight_out(
        own_half, ([all_grads], hidden), (normed_two, gate_grad), (normed_two, up_grad)
    )
    ff_wgrad, hidden = ff_small.step(two_sum.step((ff_wgrad, hidden)))
    ff_sum = lax.psum_scatter(ff_wgrad, "far", scatter_dimension=0, tiled=True)
    hidden = ff_small.step(two_sum.step(hidden))
    hidden = two_sum.finish(hidden)
    two_grad = two_sum.result

    grad_full = grad_local.astype(f32)
    dbias_part = jnp.sum(grad_full, axis=0)
    mixed_part, gain_two_part = norm_two_pull(two_grad)
    mixed_grad = grad_full + mixed_part
    obias_part = jnp.sum(mixed_grad, axis=0)
    mixed_low = mixed_grad.astype(bf16)
    mixed_other = swap(mixed_low, plan.tensor)
    hidden, mixed_low = tie(hidden, mixed_low)
    out_other = rows_out([hidden[1]], [full_down])
    out_other, hidden = tie(out_other, hidden)
    out_own = rows_out([hidden[0]], [full_down])
    out_sum = Journey(reduce_tokens(out_own, out_other, plan, token_count))
    mixed_other, out_own = tie(mixed_other, out_own)
    attn_rows = jnp.concatenate(in_order(plan.tensor, mixed_low, mixed_other), axis=0)
    order_one = plan.ctx[::-1] + plan.near + plan.far[::-1]
    order_two = [plan.core] + plan.near + plan.y[::-1] + plan.far[::-1]
    attn_rows = ff_small.finish(out_sum.step(attn_rows))
    query_proj_grad, stacked = attend_back(
        attn_rows, full_output, queries, logs, keyvalue, allowed, cosine_both, sine_both
    )
    stacked, query_proj_grad, attn_rows = tie(stacked, query_proj_grad, attn_rows)
    query_wgrad = weight_out(own_half, ([normed], [query_proj_grad]))
    for bit in reversed(plan.ctx):
        half = stacked.shape[0] // 2
        other = swap(stacked[half:].astype(bf16), bit)
        if bit == plan.core:
            other, query_wgrad, attn_rows = tie(other, query_wgrad, attn_rows)
            query_sum = Journey(reduce_rows([query_wgrad], plan, [order_one]))
            output_wgrad = weight_out(own_half, ([attn_rows], [context]))
        elif bit == plan.y[-1]:
            other, output_wgrad = query_sum.step(out_sum.step((other, output_wgrad)))
        stacked = stacked[:half] + other.astype(f32)
    mine, theirs = halves(stacked, plan.tensor, 1)
    half_grad = mine + swap(theirs.astype(bf16), plan.tensor).astype(f32)
    half_grad = jnp.where(
        is_key, rotate(half_grad[:, None, :], cosine_table, sine_table, -1.0)[:, 0], half_grad
    ).astype(bf16)
    one_part = rows_out([query_proj_grad, half_grad], [first, first], f32, [0, query_columns])
    mine, theirs = halves(one_part, plan.tensor, 0)
    theirs, half_grad, output_wgrad = tie(theirs.astype(bf16), half_grad, output_wgrad)
    other = swap(theirs, plan.tensor)
    keyvalue_wgrad = weight_out(own_half, ([normed], [half_grad]))
    other, keyvalue_wgrad, output_wgrad = out_sum.step((other, keyvalue_wgrad, output_wgrad))
    input_part, gain_one_part = norm_one_pull(mine + other.astype(f32))
    input_grad = mixed_grad + input_part
    input_grad, output_wgrad, keyvalue_wgrad = out_sum.finish(
        (input_grad, output_wgrad, keyvalue_wgrad)
    )
    block_output = (mixed + out_sum.result + full_dbias).astype(bf16)

    small = jnp.stack([gain_one_part, gain_two_part, obias_part, dbias_part], axis=0)
    small = small + swap(small, plan.tensor)
    small = jnp.pad(small.T.astype(bf16), ((0, 0), (0, LANES - 4)))
    keyvalue_wgrad = jnp.concatenate([keyvalue_wgrad, small], axis=1)
    keyvalue_sum = Journey(reduce_rows([keyvalue_wgrad], plan, [order_one]))
    input_grad = query_sum.step(input_grad)
    output_wgrad, input_grad = tie(output_wgrad, input_grad)
    output_sum = Journey(reduce_rows([output_wgrad], plan, [order_one]))
    input_grad = output_sum.step(input_grad)
    input_grad = keyvalue_sum.step(input_grad)
    ff_sum, input_grad = tie(ff_sum, input_grad)
    y_first = [plan.core] + plan.y[::-1] + plan.near[::-1]
    near_first = [plan.core] + plan.near[::-1] + plan.y[::-1]
    backs = [
        Journey(spread_back(ff_sum[:, i * block : (i + 1) * block], plan, bits))
        for i, bits in enumerate((y_first, y_first, near_first))
    ]
    input_grad = backs[0].step(input_grad)
    input_grad = backs[1].step(input_grad)
    input_grad = backs[2].step(input_grad)
    input_grad = query_sum.step(input_grad)
    input_grad = keyvalue_sum.step(input_grad)
    input_grad = finish_all([output_sum, query_sum, *backs, keyvalue_sum], input_grad)
    proj_out = output_sum.result[0]
    query_out = query_sum.result[0]
    keyvalue_out = keyvalue_sum.result[0][:, :keyvalue_columns]
    small = keyvalue_sum.result[0][:, keyvalue_columns : keyvalue_columns + 4].T
    ff_small = ff_small.result
    down_out, gate_out, up_out = (item.result[:, :ff_half].astype(f32) for item in backs)
    return (
        block_output[None],
        input_grad[None],
        small[0],
        query_out,
        keyvalue_out,
        proj_out.T,
        small[2],
        small[1],
        gate_out,
        up_out,
        down_out.T,
        ff_small[0, :ff_half],
        ff_small[1, :ff_half],
        small[3],
    )


def solution(mesh):
    near = 2
    shape = (mesh.shape["dp"] // near, near, mesh.shape["ctx"] // 2, 2, mesh.shape["tensor"])
    names = DP + CTX + ("tensor",)
    mesh = Mesh(mesh.devices.reshape(shape), names)
    plan = Plan(dict(zip(names, shape, strict=True)))
    rows = P(DP, CTX + ("tensor",), None)
    vector = P(DP_CTX)
    wide = P(DP_CTX, "tensor")
    tall = P("tensor", DP_CTX)
    units = P("tensor")
    return jax.shard_map(
        partial(local, plan),
        mesh=mesh,
        in_specs=(
            rows,
            P(DP, CTX),
            rows,
            vector,
            wide,
            wide,
            tall,
            vector,
            vector,
            wide,
            wide,
            tall,
            units,
            units,
            vector,
        ),
        out_specs=(
            rows,
            rows,
            vector,
            wide,
            wide,
            tall,
            vector,
            vector,
            wide,
            wide,
            tall,
            units,
            units,
            vector,
        ),
        check_vma=False,
    )
```
